256 devices in a mesh: layer: 32 (over y, x, core), space: 8 (over z).
Axes of the slice: x: 4, y: 4, z: 8, core: 2. Of those that a mesh axis runs over, the one named last changes fastest.
Arguments:
- start_values: float32 [32, 64, 128, 128], P('layer', None, 'space'), may hold values from -6 to 6
- weights: bfloat16 [128, 9, 4096], P('layer'), may hold values from -2.1 to 1.2
Outputs:
- coarse_values: float32 [32, 64, 128, 128], P('layer', None, 'space')
The draws below stay inside these ranges and needn't reach their ends.
All inputs are finite; a program needn't handle non-finite values.
Results may differ from the reference program's by a relative error of at most 0.025.
Values may be sent and summed in bfloat16 or wider, within the bound.
No kernel may reach another device: no remote copies, remote signals or barrier semaphores. Data moves between devices by JAX's collectives and lax.ppermute only.
A program may use at most 64 MiB of HBM per device.

```python
import math
import jax
import jax.numpy as jnp
from jax import lax

C = 64
W = 128
M = 4
NC = 32
L = 128
H = 128


def draw_weights(key, part):
    key = jax.random.fold_in(key, 11)
    rough_key, rate_key = jax.random.split(key)
    spread = 0.7 / math.sqrt(9 * C)
    rough = jnp.clip(jax.random.normal(rough_key, (L, 9, C * C), jnp.float32), -6.0, 6.0) * spread
    rates = jax.random.uniform(rate_key, (L, 1, C, 1), jnp.float32, 0.6, 0.95)
    ident = (lax.iota(jnp.int32, C)[:, None] == lax.iota(jnp.int32, C)[None, :]).astype(jnp.float32)
    diagonal = (rates * ident[None, None]).reshape(L, 1, C * C)
    profile = jnp.array([0.0, 1.0, 0.0, 0.0, -2.0, 0.0, 0.0, 1.0, 0.0], jnp.float32)
    drawn = rough + profile[None, :, None] * diagonal
    return drawn.astype(jnp.bfloat16)


def block_scale(stream_key, extent, cuts, low, top_value):
    level = 1.0
    for position, shards_of in cuts:
        steps = jax.random.uniform(jax.random.fold_in(jax.random.fold_in(stream_key, 6), position), (shards_of,), jnp.float32, low / len(cuts), top_value / len(cuts))
        level = level * jnp.repeat(jnp.exp(steps), extent[position] // shards_of).reshape((-1,) + (1,) * (len(extent) - 1 - position))
    return level


def normal_values(key, extent, scale, reach, cuts=(), held_as=jnp.bfloat16):
    entries = scale * jax.random.normal(key, extent, jnp.float32)
    if cuts:
        entries = entries * block_scale(key, extent, cuts, -0.22, 0.18)
    return jnp.clip(entries, -reach, reach).astype(held_as)


def setup_inputs(seed: int = 0) -> dict:
    arg_keys = jax.random.split(jax.random.key(seed), 3)
    return {
        "start_values": normal_values(arg_keys[0], (NC, C, H, W), 1.0, 6.0, ((0, 32), (2, 8)), jnp.float32),
        "weights": draw_weights(jax.random.fold_in(arg_keys[2], 71), 0),
    }


def convolve(field, taps):
    channels, height, breadth = field.shape
    active = jax.nn.relu(field).astype(jnp.bfloat16)
    padded = jnp.pad(active, ((0, 0), (1, 1), (1, 1)))
    accumulated = jnp.zeros((channels, height * breadth), jnp.float32)
    for row_shift in range(3):
        for col_shift in range(3):
            window = padded[:, row_shift:row_shift + height, col_shift:col_shift + breadth].reshape(channels, height * breadth)
            matrix = taps[3 * row_shift + col_shift].reshape(channels, channels)
            accumulated = accumulated + jnp.dot(matrix, window, preferred_element_type=jnp.float32)
    return accumulated.reshape(channels, height, breadth)


def advance(field, taps, step_size):
    return field + step_size * convolve(field, taps)


def reference(start_values, weights):
    kernels = weights.reshape(NC, M, 9, C * C)
    fine_size = 0.5 / M

    def whole_block(inputs):
        field, block_kernels = inputs
        for j in range(M):
            field = advance(field, block_kernels[j], fine_size)
        return field

    block_end = lax.map(whole_block, (start_values, kernels))
    relaxed = jnp.concatenate([start_values[:1], block_end[:-1]], axis=0)

    def defect_of(inputs):
        field, block_kernels = inputs
        propagated = whole_block((field, block_kernels))
        return propagated - advance(field, block_kernels[0], 0.5)

    defects = lax.map(defect_of, (relaxed, kernels))

    def coarse_turn(current, inputs):
        taps, defect = inputs
        updated = advance(current, taps, 0.5) + defect
        return updated, updated

    _, coarse_values = lax.scan(coarse_turn, start_values[0], (kernels[:, 0], defects))
    return coarse_values
```

```python
import functools
import jax
import jax.numpy as jnp
from jax import lax
from jax.experimental import pallas as pl
from jax.experimental.pallas import tpu as pltpu
from jax.sharding import PartitionSpec as P

C = 64
W = 128
TILE = 16
HALF = 8
GROUP = 8
BAND = 3 * C
RASTER = 128
BF = jnp.bfloat16
F32 = jnp.float32
VM = pl.BlockSpec(memory_space=pltpu.VMEM)
SM = pl.BlockSpec(memory_space=pltpu.SMEM)
ANY = pl.BlockSpec(memory_space=pl.ANY)
PARAMS = pltpu.CompilerParams(vmem_limit_bytes=40 * 1024 * 1024)


def build_band(band, even, odd):
    band[0:64, 0:640] = even
    band[64:128, 128:768] = odd
    band[128:192, 384:1024] = even
    band[192:256, 512:1152] = odd


def clear_band(band):
    band[...] = jnp.zeros_like(band)


def activate(state, acts, lo, hi, first_row):
    lane = lax.broadcasted_iota(jnp.int32, (C, W), 1)
    for q in range(lo, hi):
        row = first_row + q
        inside = jnp.logical_and(row >= 0, row < RASTER)
        keep = jnp.where(inside, 1.0, 0.0).astype(F32)
        a = jnp.maximum(state[q], 0.0) * keep
        left = jnp.where(lane == 0, 0.0, pltpu.roll(a, 1, 1))
        right = jnp.where(lane == W - 1, 0.0, pltpu.roll(a, W - 1, 1))
        base = q * BAND
        acts[base : base + 64, :] = left.astype(BF)
        acts[base + 64 : base + 128, :] = a.astype(BF)
        acts[base + 128 : base + 192, :] = right.astype(BF)


def convolve(band, acts, lo, hi, emit):
    starts = list(range(lo, hi, 4))
    for p in range(0, len(starts), 2):
        pair = starts[p : p + 2]
        parts = [acts[(r - 1) * BAND : (r + 5) * BAND, :] for r in pair]
        rhs = parts[0] if len(parts) == 1 else jnp.concatenate(parts, axis=1)
        y = jnp.dot(band[...], rhs, preferred_element_type=F32)
        for n, r in enumerate(pair):
            for i in range(4):
                if r + i < hi:
                    emit(r + i, y[i * 64 : (i + 1) * 64, n * W : (n + 1) * W])


def clear_tail(acts, row, rows):
    acts[row * BAND : rows * BAND, :] = jnp.zeros(((rows - row) * BAND, W), BF)


def prep_kernel(start, top, bot):
    for h in range(HALF):
        top[h] = start[pl.ds(h, C, stride=TILE), :].astype(BF)
        bot[h] = start[pl.ds(h + HALF, C, stride=TILE), :].astype(BF)


def relax_kernel(where, start, up, down, weights, out, state, acts, band):
    first_row = where[1] * TILE - 8
    clear_band(band)
    clear_tail(acts, 32, 36)
    for h in range(8):
        state[h] = up[h].astype(F32)
        state[24 + h] = down[h].astype(F32)
    for h in range(TILE):
        state[8 + h] = start[pl.ds(h, C, stride=TILE), :]
    for t in range(4):
        build_band(band, weights[t, :, 0:640], weights[t, :, 640:1280])
        activate(state, acts, t, 32 - t, first_row)
        if t < 3:
            def emit(r, y):
                state[r] = state[r] + 0.125 * y
        else:
            def emit(r, y):
                out[r - 4] = (state[r] + 0.125 * y).astype(BF)
        convolve(band, acts, 1 + t, 31 - t, emit)


def defect_kernel(where, arrived, start, up, down, weights, out, state, coarse, acts, band):
    first_row = where[1] * TILE - 4
    origin = where[0] == 0
    clear_band(band)
    clear_tail(acts, 24, 28)

    @pl.when(origin)
    def _():
        for h in range(4):
            state[h] = up[4 + h].astype(F32)
            state[20 + h] = down[h].astype(F32)
        for h in range(TILE):
            state[4 + h] = start[pl.ds(h, C, stride=TILE), :]

    @pl.when(jnp.logical_not(origin))
    def _():
        for h in range(24):
            state[h] = arrived[h].astype(F32)

    subtract = jnp.where(origin, 0.0, 1.0).astype(F32)
    for t in range(4):
        build_band(band, weights[t, :, 0:640], weights[t, :, 640:1280])
        activate(state, acts, t, 24 - t, first_row)
        if t == 0:
            def emit(r, y):
                u = state[r]
                if 4 <= r < 20:
                    coarse[r - 4] = (u + 0.5 * y) * subtract
                state[r] = u + 0.125 * y
        elif t < 3:
            def emit(r, y):
                state[r] = state[r] + 0.125 * y
        else:
            def emit(r, y):
                out[r - 4] = (state[r] + 0.125 * y - coarse[r - 4]).astype(BF)
        convolve(band, acts, 1 + t, 23 - t, emit)


def slot_of(where, d, swapped):
    x, c = where[2], where[3]
    return 2 * lax.rem(x - d + 4, 4) + (1 - c if swapped else c)


OFFSETS = [0, 7, 13, 18, 22, 25, 27, 28]


def pack_kernel(where, *refs):
    pieces, out, sem = refs[:8], refs[8], refs[9]
    c = where[3]
    for d in range(4):
        for swapped in (0, 1):
            piece = pieces[2 * d + swapped]
            slot = slot_of(where, d, swapped)
            for j in range(7):
                count = 7 - j

                @pl.when(slot == j)
                def _():
                    begin = jnp.where(c == 0, TILE - count, 0)
                    pltpu.make_async_copy(
                        piece.at[pl.ds(begin, count)], out.at[pl.ds(OFFSETS[j], count)], sem
                    ).start()

    pltpu.make_async_copy(out, out, sem).wait()


def coarse_kernel(turn, where, *refs):
    pieces = refs[:8]
    edges, weights, own, other, halo = refs[8:13]
    sent, mine, theirs = refs[15:18]
    state, acts, band, defects, sems = refs[18:]
    x, c = where[2], where[3]
    first_row = where[1] * TILE - 8 + 8 * c
    mine[...] = refs[13][...]
    theirs[...] = refs[14][...]

    @pl.when(where[4] != turn)
    def _():
        sent[...] = jnp.zeros_like(sent)

    @pl.when(where[4] == turn)
    def _():
        for d in range(4):
            for swapped in (0, 1):
                slot = slot_of(where, d, swapped)
                pltpu.make_async_copy(
                    pieces[2 * d + swapped], defects.at[slot, pl.ds(8 - 8 * c, TILE)], sems.at[slot]
                ).start()
        for j in range(7):
            count = 7 - j
            begin = jnp.where(c == 0, 1 + j, TILE)
            pltpu.make_async_copy(
                edges.at[pl.ds(OFFSETS[j], count)], defects.at[j, pl.ds(begin, count)], sems.at[j]
            ).start()
        clear_band(band)
        clear_tail(acts, 24, 28)
        if turn == 0:
            for h in range(24):
                state[h] = jnp.zeros((C, W), F32)
        else:
            for h in range(8):
                state[8 + h] = own[h].astype(F32)

            @pl.when(c == 0)
            def _():
                for h in range(8):
                    state[h] = halo[h].astype(F32)
                    state[16 + h] = other[h].astype(F32)

            @pl.when(c != 0)
            def _():
                for h in range(8):
                    state[h] = other[h].astype(F32)
                    state[16 + h] = halo[h].astype(F32)

        for j in range(GROUP):
            build_band(band, weights[j, :, 0:640], weights[j, :, 640:1280])
            activate(state, acts, j, 24 - j, first_row)
            landed = defects.at[j, pl.ds(0, TILE + 7 - j)]
            pltpu.make_async_copy(landed, landed, sems.at[j]).wait()

            def emit(r, y):
                state[r] = state[r] + 0.5 * y + defects[j, r].astype(F32)

            convolve(band, acts, 1 + j, 23 - j, emit)

            @pl.when(x == j // 2)
            def _():
                @pl.when(c == j % 2)
                def _():
                    for h in range(8):
                        mine[h] = state[8 + h]

                @pl.when(c != j % 2)
                def _():
                    for h in range(8):
                        theirs[h] = state[8 + h].astype(BF)

        for h in range(8):
            sent[h] = state[8 + h].astype(BF)


def finish_kernel(where, mine, arrived, out):
    c = where[3]

    def put(lo_rows, hi_rows):
        for h in range(8):
            out[pl.ds(h, C, stride=TILE), :] = lo_rows(h)
            out[pl.ds(h + 8, C, stride=TILE), :] = hi_rows(h)

    @pl.when(c == 0)
    def _():
        put(lambda h: mine[h], lambda h: arrived[h].astype(F32))

    @pl.when(c != 0)
    def _():
        put(lambda h: arrived[h].astype(F32), lambda h: mine[h])


def rows_of(n, dtype=BF):
    return jax.ShapeDtypeStruct((n, C, W), dtype)


def on_device(start_values, weights):
    layer = lax.axis_index("layer")
    space = lax.axis_index("space")
    blocks = lax.axis_size("layer")
    tiles = lax.axis_size("space")
    axes = ("layer", "space")
    x = lax.rem(layer, 8) // 2
    c = lax.rem(layer, 2)
    where = jnp.stack([layer, space, x, c, layer // GROUP]).astype(jnp.int32)
    start = start_values.reshape(C * TILE, W)

    def at(l, s):
        return l * tiles + s

    top, bot = pl.pallas_call(
        prep_kernel, out_shape=(rows_of(8), rows_of(8)), in_specs=[VM], out_specs=(VM, VM), compiler_params=PARAMS
    )(start)
    up = lax.ppermute(bot, "space", [(s, (s + 1) % tiles) for s in range(tiles)])
    down = lax.ppermute(top, "space", [((s + 1) % tiles, s) for s in range(tiles)])

    flat = weights.reshape(4, 9, C, C).transpose(0, 2, 1, 3).reshape(4, C, 9 * C)
    bands = jnp.concatenate(
        [jnp.pad(flat, ((0, 0), (0, 0), (0, 64))), jnp.pad(flat, ((0, 0), (0, 0), (64, 0)))], axis=2
    )
    groups = [list(range(i, i + GROUP)) for i in range(0, blocks, GROUP)]
    coarse_bands = lax.all_gather(bands[0], "layer", axis_index_groups=groups)

    block_end = pl.pallas_call(
        relax_kernel,
        out_shape=rows_of(24),
        in_specs=[SM, VM, VM, VM, VM],
        out_specs=VM,
        scratch_shapes=[
            pltpu.VMEM((32, C, W), F32),
            pltpu.VMEM((36 * BAND, W), BF),
            pltpu.VMEM((256, 6 * BAND), BF),
        ],
        compiler_params=PARAMS,
    )(where, start, up, down, bands)
    arrived = lax.ppermute(block_end, "layer", [(l, (l + 1) % blocks) for l in range(blocks)])
    defect = pl.pallas_call(
        defect_kernel,
        out_shape=rows_of(16),
        in_specs=[SM, VM, VM, VM, VM, VM],
        out_specs=VM,
        scratch_shapes=[
            pltpu.VMEM((24, C, W), F32),
            pltpu.VMEM((16, C, W), F32),
            pltpu.VMEM((28 * BAND, W), BF),
            pltpu.VMEM((256, 6 * BAND), BF),
        ],
        compiler_params=PARAMS,
    )(where, arrived, start, up, down, bands)

    def around(d):
        pairs = [(l, l // 8 * 8 + (l % 8 + 2 * d) % 8) for l in range(blocks)]
        return lax.ppermute(defect, "layer", pairs)

    swap = [(l, l ^ 1) for l in range(blocks)]
    pieces = []
    for piece in (defect, around(1), around(2), around(3)):
        pieces += [piece, lax.ppermute(piece, "layer", swap)]
    packed = pl.pallas_call(
        pack_kernel,
        out_shape=rows_of(28),
        in_specs=[SM] + [ANY] * 8,
        out_specs=ANY,
        scratch_shapes=[pltpu.SemaphoreType.DMA],
        compiler_params=PARAMS,
    )(where, *pieces)
    edge_pairs = [
        (at(l, s), at(l, (s + 1) % tiles if l % 2 == 0 else (s - 1) % tiles)) for l in range(blocks) for s in range(tiles)
    ]
    edges = lax.ppermute(packed, axes, edge_pairs)

    own = other = halo = jnp.zeros((8, C, W), BF)
    mine = jnp.zeros((8, C, W), F32)
    theirs = jnp.zeros((8, C, W), BF)
    turns = blocks // GROUP
    for turn in range(turns):
        sent, mine, theirs = pl.pallas_call(
            functools.partial(coarse_kernel, turn),
            out_shape=(rows_of(8), rows_of(8, F32), rows_of(8)),
            in_specs=[SM] + [ANY] * 9 + [VM] * 6,
            out_specs=(VM, VM, VM),
            scratch_shapes=[
                pltpu.VMEM((24, C, W), F32),
                pltpu.VMEM((28 * BAND, W), BF),
                pltpu.VMEM((256, 6 * BAND), BF),
                pltpu.VMEM((GROUP, 24, C, W), BF),
                pltpu.SemaphoreType.DMA((GROUP,)),
            ],
            input_output_aliases={14: 1, 15: 2},
            compiler_params=PARAMS,
        )(where, *pieces, edges, coarse_bands, own, other, halo, mine, theirs)
        if turn + 1 < turns:
            senders = range(GROUP * turn, GROUP * (turn + 1))
            own = lax.ppermute(sent, axes, [(at(l, s), at(l + 8, s)) for l in senders for s in range(tiles)])
            other = lax.ppermute(sent, axes, [(at(l, s), at((l ^ 1) + 8, s)) for l in senders for s in range(tiles)])
            halo = lax.ppermute(
                sent,
                axes,
                [
                    (at(l, s), at((l ^ 1) + 8, s + (1 if l % 2 else -1)))
                    for l in senders
                    for s in range(tiles)
                    if 0 <= s + (1 if l % 2 else -1) < tiles
                ],
            )
    arrived = lax.ppermute(theirs, "layer", swap)
    result = pl.pallas_call(
        finish_kernel,
        out_shape=jax.ShapeDtypeStruct((C * TILE, W), F32),
        in_specs=[SM, VM, VM],
        out_specs=VM,
        compiler_params=PARAMS,
    )(where, mine, arrived)
    return result.reshape(1, C, TILE, W)


def solution(mesh):
    placed = (P("layer", None, "space", None), P("layer", None, None))
    return jax.shard_map(
        on_device,
        mesh=mesh,
        in_specs=placed,
        out_specs=P("layer", None, "space", None),
        check_vma=False,
    )
```

```python
import functools
import jax
import jax.numpy as jnp
from jax import lax
from jax.experimental import pallas as pl
from jax.experimental.pallas import tpu as pltpu
from jax.sharding import PartitionSpec as P

C = 64
W = 128
TILE = 16
HALF = 8
GROUP = 8
BAND = 3 * C
RASTER = 128
BF = jnp.bfloat16
F32 = jnp.float32
VM = pl.BlockSpec(memory_space=pltpu.VMEM)
SM = pl.BlockSpec(memory_space=pltpu.SMEM)
ANY = pl.BlockSpec(memory_space=pl.ANY)
PARAMS = pltpu.CompilerParams(vmem_limit_bytes=40 * 1024 * 1024)


def build_band(band, taps):
    for i in range(4):
        band[i * C : (i + 1) * C, i * BAND : (i + 3) * BAND] = taps


def build_band_wide(band, taps):
    even = taps[:, 0:640]
    odd = taps[:, 640:1280]
    band[0:64, 0:640] = even
    band[64:128, 128:768] = odd
    band[128:192, 384:1024] = even
    band[192:256, 512:1152] = odd


def clear_band(band):
    band[...] = jnp.zeros_like(band)


def activate_row(value, acts, q, first_row):
    lane = lax.broadcasted_iota(jnp.int32, (C, W), 1)
    row = first_row + q
    inside = jnp.logical_and(row >= 0, row < RASTER)
    keep = jnp.where(inside, 1.0, 0.0).astype(F32)
    a = jnp.maximum(value, 0.0) * keep
    left = jnp.where(lane == 0, 0.0, pltpu.roll(a, 1, 1))
    right = jnp.where(lane == W - 1, 0.0, pltpu.roll(a, W - 1, 1))
    base = q * BAND
    acts[base : base + 64, :] = left.astype(BF)
    acts[base + 64 : base + 128, :] = a.astype(BF)
    acts[base + 128 : base + 192, :] = right.astype(BF)


def activate(state, acts, lo, hi, first_row):
    for q in range(lo, hi):
        activate_row(state[q], acts, q, first_row)


def convolve(band, acts, lo, hi, emit):
    starts = list(range(lo, hi, 4))
    for p in range(0, len(starts), 2):
        pair = starts[p : p + 2]
        parts = [acts[(r - 1) * BAND : (r + 5) * BAND, :] for r in pair]
        rhs = parts[0] if len(parts) == 1 else jnp.concatenate(parts, axis=1)
        y = jnp.dot(band[...], rhs, preferred_element_type=F32)
        for n, r in enumerate(pair):
            for i in range(4):
                if r + i < hi:
                    emit(r + i, y[i * 64 : (i + 1) * 64, n * W : (n + 1) * W])


def clear_tail(acts, row, rows):
    acts[row * BAND : rows * BAND, :] = jnp.zeros(((rows - row) * BAND, W), BF)


def prep_kernel(start, tile, top, bot, top4, bot4):
    for h in range(TILE):
        row = start[pl.ds(h, C, stride=TILE), :].astype(BF)
        tile[h] = row
        if h < 8:
            top[h] = row
        else:
            bot[h - 8] = row
        if h < 4:
            top4[h] = row
        if h >= 12:
            bot4[h - 12] = row


def defect_kernel(where, mid, up, down, tile, up4, down4, before, taps, out, state, coarse, acts, acts2, band):
    first_row = where[1] * TILE - 8
    origin = where[0] == 0
    both = (acts, acts2)
    clear_band(band)
    clear_tail(acts, 28, 36)

    @pl.when(origin)
    def _():
        for h in range(4):
            state[4 + h] = up4[h].astype(F32)
            state[24 + h] = down4[h].astype(F32)
        for h in range(TILE):
            state[8 + h] = tile[h].astype(F32)
        activate(state, acts, 4, 28, first_row)

    @pl.when(jnp.logical_not(origin))
    def _():
        for h in range(8):
            state[h] = up[h].astype(F32)
            state[24 + h] = down[h].astype(F32)
        for h in range(TILE):
            state[8 + h] = mid[h].astype(F32)
        activate(state, acts, 0, 32, first_row)
        for t in range(4):
            build_band(band, before[t])

            def emit(r, y):
                v = state[r] + 0.125 * y
                state[r] = v
                activate_row(v, both[(t + 1) % 2], r, first_row)

            convolve(band, both[t % 2], 1 + t, 31 - t, emit)

    subtract = jnp.where(origin, 0.0, 1.0).astype(F32)
    for t in range(4):
        build_band(band, taps[t])

        def emit(r, y):
            u = state[r]
            v = u + 0.125 * y
            if t == 0 and 8 <= r < 24:
                coarse[r - 8] = (u + 0.5 * y) * subtract
            if t < 3:
                state[r] = v
                activate_row(v, both[(t + 1) % 2], r, first_row)
            else:
                out[r - 8] = (v - coarse[r - 8]).astype(BF)

        convolve(band, both[t % 2], 5 + t, 27 - t, emit)


def slot_of(where, d, swapped):
    x, c = where[2], where[3]
    return 2 * lax.rem(x - d + 4, 4) + (1 - c if swapped else c)


OFFSETS = [0, 7, 13, 18, 22, 25, 27, 28]


def arrange_kernel(where, *refs):
    pieces, ordered, packed = refs[:8], refs[8], refs[9]
    c = where[3]
    for d in range(4):
        for swapped in (0, 1):
            slot = slot_of(where, d, swapped)
            ordered[pl.ds(slot, 1)] = pieces[2 * d + swapped][...][None]
    for j in range(7):
        count = 7 - j
        begin = jnp.where(c == 0, TILE - count, 0)
        packed[OFFSETS[j] : OFFSETS[j + 1]] = ordered[j, pl.ds(begin, count)]


def coarse_kernel(turn, where, ordered, edges, weights, own, other, halo, mine_in, theirs_in, sent, mine, theirs, state, acts, acts2, band, past):
    x, c = where[2], where[3]
    first_row = where[1] * TILE - 8 + 8 * c
    both = (acts, acts2)

    @pl.when(where[4] != turn)
    def _():
        mine[...] = mine_in[...]
        theirs[...] = theirs_in[...]
        sent[...] = jnp.zeros_like(sent)

    @pl.when(where[4] == turn)
    def _():
        clear_band(band)
        clear_tail(acts, 24, 28)
        for h in range(24):
            if turn == 0:
                v = jnp.zeros((C, W), F32)
            elif h < 8:
                v = jnp.where(c == 0, halo[h].astype(F32), other[h].astype(F32))
            elif h < 16:
                v = own[h - 8].astype(F32)
            else:
                v = jnp.where(c == 0, other[h - 16].astype(F32), halo[h - 16].astype(F32))
            state[h] = v
            activate_row(v, acts, h, first_row)

        for j in range(GROUP):
            build_band_wide(band, weights[j])

            def emit(r, y):
                if 8 <= r < 16:
                    e = ordered[j, r - 8 + 8 * c]
                elif r < 8:
                    e = jnp.where(c == 0, edges[OFFSETS[j] + r - 1 - j], ordered[j, r])
                else:
                    e = jnp.where(c == 0, ordered[j, r - 8], edges[OFFSETS[j] + r - 16])
                v = state[r] + 0.5 * y + e.astype(F32)
                if j < GROUP - 1:
                    state[r] = v
                    activate_row(v, both[(j + 1) % 2], r, first_row)
                else:
                    sent[r - 8] = v.astype(BF)
                if 8 <= r < 16:
                    past[j, r - 8] = v

            convolve(band, both[j % 2], 1 + j, 23 - j, emit)

        mine[...] = past[2 * x + c]
        theirs[...] = past[2 * x + 1 - c].astype(BF)


def finish_kernel(where, mine, arrived, out):
    c = where[3]

    def put(lo_rows, hi_rows):
        for h in range(8):
            out[pl.ds(h, C, stride=TILE), :] = lo_rows(h)
            out[pl.ds(h + 8, C, stride=TILE), :] = hi_rows(h)

    @pl.when(c == 0)
    def _():
        put(lambda h: mine[h], lambda h: arrived[h].astype(F32))

    @pl.when(c != 0)
    def _():
        put(lambda h: arrived[h].astype(F32), lambda h: mine[h])


def rows_of(n, dtype=BF):
    return jax.ShapeDtypeStruct((n, C, W), dtype)


def on_device(start_values, weights):
    layer = lax.axis_index("layer")
    space = lax.axis_index("space")
    blocks = lax.axis_size("layer")
    tiles = lax.axis_size("space")
    axes = ("layer", "space")
    x = lax.rem(layer, 8) // 2
    c = lax.rem(layer, 2)
    where = jnp.stack([layer, space, x, c, layer // GROUP]).astype(jnp.int32)
    start = start_values.reshape(C * TILE, W)

    def at(l, s):
        return l * tiles + s

    tile, top, bot, top4, bot4 = pl.pallas_call(
        prep_kernel,
        out_shape=(rows_of(16), rows_of(8), rows_of(8), rows_of(4), rows_of(4)),
        in_specs=[VM],
        out_specs=(VM,) * 5,
        compiler_params=PARAMS,
    )(start)
    everywhere = [(l, s) for l in range(blocks) for s in range(tiles)]

    def shifted(piece, dl, ds):
        return lax.ppermute(piece, axes, [(at(l, s), at((l + dl) % blocks, (s + ds) % tiles)) for l, s in everywhere])

    mid = shifted(tile, 1, 0)
    up = shifted(bot, 1, 1)
    down = shifted(top, 1, -1)
    up4 = shifted(bot4, 0, 1)
    down4 = shifted(top4, 0, -1)

    flat = weights.reshape(4, 9, C, C).transpose(0, 2, 1, 3).reshape(4, C, 9 * C)
    before = shifted(flat, 1, 0)
    groups = [list(range(i, i + GROUP)) for i in range(0, blocks, GROUP)]
    wide = jnp.concatenate([jnp.pad(flat[0], ((0, 0), (0, 64))), jnp.pad(flat[0], ((0, 0), (64, 0)))], axis=1)
    coarse_bands = lax.all_gather(wide, "layer", axis_index_groups=groups)

    defect = pl.pallas_call(
        defect_kernel,
        out_shape=rows_of(16),
        in_specs=[SM] + [VM] * 8,
        out_specs=VM,
        scratch_shapes=[
            pltpu.VMEM((32, C, W), F32),
            pltpu.VMEM((16, C, W), F32),
            pltpu.VMEM((36 * BAND, W), BF),
            pltpu.VMEM((36 * BAND, W), BF),
            pltpu.VMEM((256, 6 * BAND), BF),
        ],
        compiler_params=PARAMS,
    )(where, mid, up, down, tile, up4, down4, before, flat)

    def around(piece, d, cores):
        pairs = [(l, l // 8 * 8 + (l % 8 + 2 * d) % 8) for l in range(blocks) if l % 2 in cores]
        return lax.ppermute(piece, "layer", pairs)

    swap = [(l, l ^ 1) for l in range(blocks)]
    ahead = around(defect, 1, (0, 1))
    behind = around(defect, 3, (0, 1))
    across = jnp.where(c == 0, around(defect, 2, (0,)), around(behind, 3, (1,)))
    pieces = []
    for piece in (defect, ahead, across, behind):
        pieces += [piece, lax.ppermute(piece, "layer", swap)]
    ordered, packed = pl.pallas_call(
        arrange_kernel,
        out_shape=(jax.ShapeDtypeStruct((GROUP, TILE, C, W), BF), rows_of(28)),
        in_specs=[SM] + [VM] * 8,
        out_specs=(VM, VM),
        compiler_params=PARAMS,
    )(where, *pieces)
    edge_pairs = [
        (at(l, s), at(l, (s + 1) % tiles if l % 2 == 0 else (s - 1) % tiles)) for l in range(blocks) for s in range(tiles)
    ]
    edges = lax.ppermute(packed, axes, edge_pairs)

    own = other = halo = jnp.zeros((8, C, W), BF)
    mine = jnp.zeros((8, C, W), F32)
    theirs = jnp.zeros((8, C, W), BF)
    turns = blocks // GROUP
    for turn in range(turns):
        sent, mine, theirs = pl.pallas_call(
            functools.partial(coarse_kernel, turn),
            out_shape=(rows_of(8), rows_of(8, F32), rows_of(8)),
            in_specs=[SM] + [VM] * 8,
            out_specs=(VM, VM, VM),
            scratch_shapes=[
                pltpu.VMEM((24, C, W), F32),
                pltpu.VMEM((28 * BAND, W), BF),
                pltpu.VMEM((28 * BAND, W), BF),
                pltpu.VMEM((256, 6 * BAND), BF),
                pltpu.VMEM((GROUP, 8, C, W), F32),
            ],
            input_output_aliases={7: 1, 8: 2},
            compiler_params=PARAMS,
        )(where, ordered, edges, coarse_bands, own, other, halo, mine, theirs)
        if turn + 1 < turns:
            senders = range(GROUP * turn, GROUP * (turn + 1))
            own = lax.ppermute(sent, axes, [(at(l, s), at(l + 8, s)) for l in senders for s in range(tiles)])
            other = lax.ppermute(sent, axes, [(at(l, s), at((l ^ 1) + 8, s)) for l in senders for s in range(tiles)])
            halo = lax.ppermute(
                sent,
                axes,
                [
                    (at(l, s), at((l ^ 1) + 8, s + (1 if l % 2 else -1)))
                    for l in senders
                    for s in range(tiles)
                    if 0 <= s + (1 if l % 2 else -1) < tiles
                ],
            )
    arrived = lax.ppermute(theirs, "layer", swap)
    result = pl.pallas_call(
        finish_kernel,
        out_shape=jax.ShapeDtypeStruct((C * TILE, W), F32),
        in_specs=[SM, VM, VM],
        out_specs=VM,
        compiler_params=PARAMS,
    )(where, mine, arrived)
    return result.reshape(1, C, TILE, W)


def solution(mesh):
    placed = (P("layer", None, "space", None), P("layer", None, None))
    return jax.shard_map(
        on_device,
        mesh=mesh,
        in_specs=placed,
        out_specs=P("layer", None, "space", None),
        check_vma=False,
    )
```

```python
import functools
import jax
import jax.numpy as jnp
from jax import lax
from jax.experimental import pallas as pl
from jax.experimental.pallas import tpu as pltpu
from jax.sharding import PartitionSpec as P

C = 64
W = 128
TILE = 16
GROUP = 8
BAND = 3 * C
RASTER = 128
BF = jnp.bfloat16
F32 = jnp.float32
VM = pl.BlockSpec(memory_space=pltpu.VMEM)
SM = pl.BlockSpec(memory_space=pltpu.SMEM)
PARAMS = pltpu.CompilerParams(vmem_limit_bytes=12 * 1024 * 1024)


def build_band(band, taps):
    for i in range(2):
        band[i * C : (i + 1) * C, i * BAND : (i + 3) * BAND] = taps


def clear_band(band):
    band[...] = jnp.zeros_like(band)


def activate_row(value, acts, q, first_row):
    lane = lax.broadcasted_iota(jnp.int32, (C, W), 1)
    row = first_row + q
    inside = jnp.logical_and(row >= 0, row < RASTER)
    keep = jnp.where(inside, 1.0, 0.0).astype(F32)
    a = (jnp.maximum(value, 0.0) * keep).astype(BF)
    zero = jnp.zeros((), BF)
    base = q * BAND
    acts[base : base + 64, :] = jnp.where(lane == 0, zero, pltpu.roll(a, 1, 1))
    acts[base + 64 : base + 128, :] = a
    acts[base + 128 : base + 192, :] = jnp.where(lane == W - 1, zero, pltpu.roll(a, W - 1, 1))


def activate(state, acts, lo, hi, first_row):
    for q in range(lo, hi):
        activate_row(state[q], acts, q, first_row)


def convolve(band, acts, lo, hi, emit):
    for r in range(lo, hi, 4):
        pair = [q for q in (r, r + 2) if q < hi]
        parts = [acts[(q - 1) * BAND : (q + 3) * BAND, :] for q in pair]
        rhs = parts[0] if len(parts) == 1 else jnp.concatenate(parts, axis=1)
        y = jnp.dot(band[...], rhs, preferred_element_type=F32)
        for n, q in enumerate(pair):
            for i in range(2):
                emit(q + i, y[i * C : (i + 1) * C, n * W : (n + 1) * W])


def prep_kernel(start, tile, top, bot, top4, bot4):
    for h in range(TILE):
        row = start[pl.ds(h, C, stride=TILE), :].astype(BF)
        tile[h] = row
        if h < 8:
            top[h] = row
        else:
            bot[h - 8] = row
        if h < 4:
            top4[h] = row
        if h >= 12:
            bot4[h - 12] = row


def defect_kernel(where, mid, up, down, tile, up4, down4, before, taps, out, state, coarse, acts, acts2, band):
    first_row = where[1] * TILE - 8
    origin = where[0] == 0
    both = (acts, acts2)
    clear_band(band)

    @pl.when(origin)
    def _():
        for h in range(4):
            state[4 + h] = up4[h].astype(F32)
            state[24 + h] = down4[h].astype(F32)
        for h in range(TILE):
            state[8 + h] = tile[h].astype(F32)
        activate(state, acts, 4, 28, first_row)

    @pl.when(jnp.logical_not(origin))
    def _():
        for h in range(8):
            state[h] = up[h].astype(F32)
            state[24 + h] = down[h].astype(F32)
        for h in range(TILE):
            state[8 + h] = mid[h].astype(F32)
        activate(state, acts, 0, 32, first_row)
        for t in range(4):
            build_band(band, before[t])

            def emit(r, y):
                v = state[r] + 0.125 * y
                state[r] = v
                activate_row(v, both[(t + 1) % 2], r, first_row)

            convolve(band, both[t % 2], 1 + t, 31 - t, emit)

    subtract = jnp.where(origin, 0.0, 1.0).astype(F32)
    for t in range(4):
        build_band(band, taps[t])

        def emit(r, y):
            u = state[r]
            v = u + 0.125 * y
            if t == 0 and 8 <= r < 24:
                coarse[r - 8] = (u + 0.5 * y) * subtract
            if t < 3:
                state[r] = v
                activate_row(v, both[(t + 1) % 2], r, first_row)
            else:
                out[r - 8] = (v - coarse[r - 8]).astype(BF)

        convolve(band, both[t % 2], 5 + t, 27 - t, emit)


def slot_of(where, d, swapped):
    x, c = where[2], where[3]
    return 2 * lax.rem(x - d + 4, 4) + (1 - c if swapped else c)


OFFSETS = [0, 7, 13, 18, 22, 25, 27, 28]


def arrange_kernel(where, *refs):
    pieces, ordered, packed = refs[:10], refs[10], refs[11]
    c = where[3]
    places = [(0, 0, 16), (1, 0, 16), (3, 0, 16), (2, 0, 8), (2, 8, 8)]
    for n, (d, begin, count) in enumerate(places):
        for swapped in (0, 1):
            slot = slot_of(where, d, swapped)
            ordered[pl.ds(slot, 1), begin : begin + count] = pieces[2 * n + swapped][...][None]
    for j in range(7):
        count = 7 - j
        begin = jnp.where(c == 0, TILE - count, 0)
        packed[OFFSETS[j] : OFFSETS[j + 1]] = ordered[j, pl.ds(begin, count)]


def coarse_kernel(
    turn, where, ordered, edges, w0, w1, w2, w3, own, other, halo, mine_in, theirs_in,
    sent, mine, theirs, state, acts, acts2, band, past, taps
):
    x, c = where[2], where[3]
    first_row = where[1] * TILE - 8 + 8 * c
    both = (acts, acts2)

    @pl.when(where[4] != turn)
    def _():
        mine[...] = mine_in[...]
        theirs[...] = theirs_in[...]
        sent[...] = jnp.zeros_like(sent)

    @pl.when(where[4] == turn)
    def _():
        clear_band(band)
        for h in range(24):
            if turn == 0:
                v = jnp.zeros((C, W), F32)
            elif h < 8:
                v = jnp.where(c == 0, halo[h].astype(F32), other[h].astype(F32))
            elif h < 16:
                v = own[h - 8].astype(F32)
            else:
                v = jnp.where(c == 0, other[h - 16].astype(F32), halo[h - 16].astype(F32))
            state[h] = v
            activate_row(v, acts, h, first_row)
        for d, pair in enumerate((w0, w1, w2, w3)):
            for swapped in (0, 1):
                taps[slot_of(where, d, swapped)] = pair[swapped]

        for j in range(GROUP):
            build_band(band, taps[j])

            def emit(r, y):
                if 8 <= r < 16:
                    e = ordered[j, r - 8 + 8 * c]
                elif r < 8:
                    e = jnp.where(c == 0, edges[OFFSETS[j] + r - 1 - j], ordered[j, r])
                else:
                    e = jnp.where(c == 0, ordered[j, r - 8], edges[OFFSETS[j] + r - 16])
                v = state[r] + 0.5 * y + e.astype(F32)
                if j < GROUP - 1:
                    state[r] = v
                    activate_row(v, both[(j + 1) % 2], r, first_row)
                else:
                    sent[r - 8] = v.astype(BF)
                if 8 <= r < 16:
                    past[j, r - 8] = v

            convolve(band, both[j % 2], 1 + j, 23 - j, emit)

        mine[...] = past[2 * x + c]
        theirs[...] = past[2 * x + 1 - c].astype(BF)


def finish_kernel(where, mine, arrived, out):
    c = where[3]

    def put(lo_rows, hi_rows):
        for h in range(8):
            out[pl.ds(h, C, stride=TILE), :] = lo_rows(h)
            out[pl.ds(h + 8, C, stride=TILE), :] = hi_rows(h)

    @pl.when(c == 0)
    def _():
        put(lambda h: mine[h], lambda h: arrived[h].astype(F32))

    @pl.when(c != 0)
    def _():
        put(lambda h: arrived[h].astype(F32), lambda h: mine[h])


def rows_of(n, dtype=BF):
    return jax.ShapeDtypeStruct((n, C, W), dtype)


def on_device(start_values, weights):
    layer = lax.axis_index("layer")
    space = lax.axis_index("space")
    blocks = lax.axis_size("layer")
    tiles = lax.axis_size("space")
    axes = ("layer", "space")
    x = lax.rem(layer, 8) // 2
    c = lax.rem(layer, 2)
    where = jnp.stack([layer, space, x, c, layer // GROUP]).astype(jnp.int32)
    start = start_values.reshape(C * TILE, W)

    def at(l, s):
        return l * tiles + s

    tile, top, bot, top4, bot4 = pl.pallas_call(
        prep_kernel,
        out_shape=(rows_of(16), rows_of(8), rows_of(8), rows_of(4), rows_of(4)),
        in_specs=[VM],
        out_specs=(VM,) * 5,
        compiler_params=PARAMS,
    )(start)
    everywhere = [(l, s) for l in range(blocks) for s in range(tiles)]

    def shifted(piece, dl, ds):
        return lax.ppermute(piece, axes, [(at(l, s), at((l + dl) % blocks, (s + ds) % tiles)) for l, s in everywhere])

    mid = shifted(tile, 1, 0)
    up = shifted(bot, 1, 1)
    down = shifted(top, 1, -1)
    up4 = shifted(bot4, 0, 1)
    down4 = shifted(top4, 0, -1)

    flat = weights.reshape(4, 9, C, C).transpose(0, 2, 1, 3).reshape(4, C, 9 * C)
    before = shifted(flat, 1, 0)
    swap = [(l, l ^ 1) for l in range(blocks)]
    first, mid, before = lax.optimization_barrier((flat[0], mid, before))

    def around(piece, d, cores=(0, 1)):
        pairs = [(l, l // 8 * 8 + (l % 8 + 2 * d) % 8) for l in range(blocks) if l % 2 in cores]
        return lax.ppermute(piece, "layer", pairs)

    pair = jnp.stack([first, lax.ppermute(first, "layer", swap)])

    defect = pl.pallas_call(
        defect_kernel,
        out_shape=rows_of(16),
        in_specs=[SM] + [VM] * 8,
        out_specs=VM,
        scratch_shapes=[
            pltpu.VMEM((32, C, W), F32),
            pltpu.VMEM((16, C, W), F32),
            pltpu.VMEM((32 * BAND, W), BF),
            pltpu.VMEM((32 * BAND, W), BF),
            pltpu.VMEM((2 * C, 4 * BAND), BF),
        ],
        cost_estimate=pl.CostEstimate(flops=2_000_000_000, bytes_accessed=4_000_000, transcendentals=0),
        compiler_params=PARAMS,
    )(where, mid, up, down, tile, up4, down4, before, flat)

    ahead = around(defect, 1)
    behind = around(defect, 3)
    across = around(defect[:8], 2)
    across2 = around(behind[8:], 3)
    pieces = []
    for piece in (defect, ahead, behind, across, across2):
        pieces += [piece, lax.ppermute(piece, "layer", swap)]
    ordered, packed = pl.pallas_call(
        arrange_kernel,
        out_shape=(jax.ShapeDtypeStruct((GROUP, TILE, C, W), BF), rows_of(28)),
        in_specs=[SM] + [VM] * 10,
        out_specs=(VM, VM),
        compiler_params=PARAMS,
    )(where, *pieces)
    edge_pairs = [
        (at(l, s), at(l, (s + 1) % tiles if l % 2 == 0 else (s - 1) % tiles)) for l in range(blocks) for s in range(tiles)
    ]
    pair, packed = lax.optimization_barrier((pair, packed))
    edges = lax.ppermute(packed, axes, edge_pairs)
    coarse_taps = [pair, around(pair, 1), around(pair, 2), around(pair, 3)]

    own = other = halo = jnp.zeros((8, C, W), BF)
    mine = jnp.zeros((8, C, W), F32)
    theirs = jnp.zeros((8, C, W), BF)
    turns = blocks // GROUP
    for turn in range(turns):
        sent, mine, theirs = pl.pallas_call(
            functools.partial(coarse_kernel, turn),
            out_shape=(rows_of(8), rows_of(8, F32), rows_of(8)),
            in_specs=[SM] + [VM] * 11,
            out_specs=(VM, VM, VM),
            scratch_shapes=[
                pltpu.VMEM((24, C, W), F32),
                pltpu.VMEM((24 * BAND, W), BF),
                pltpu.VMEM((24 * BAND, W), BF),
                pltpu.VMEM((2 * C, 4 * BAND), BF),
                pltpu.VMEM((GROUP, 8, C, W), F32),
                pltpu.VMEM((GROUP, C, 9 * C), BF),
            ],
            input_output_aliases={10: 1, 11: 2},
            compiler_params=PARAMS,
        )(where, ordered, edges, *coarse_taps, own, other, halo, mine, theirs)
        if turn + 1 < turns:
            own = lax.ppermute(sent, "layer", [(l, (l + 8) % blocks) for l in range(blocks)])
            other = lax.ppermute(own, "layer", swap)
            halo = lax.ppermute(
                sent,
                axes,
                [(at(l, s), at(((l ^ 1) + 8) % blocks, (s + (1 if l % 2 else -1)) % tiles)) for l, s in everywhere],
            )
    arrived = lax.ppermute(theirs, "layer", swap)
    result = pl.pallas_call(
        finish_kernel,
        out_shape=jax.ShapeDtypeStruct((C * TILE, W), F32),
        in_specs=[SM, VM, VM],
        out_specs=VM,
        compiler_params=PARAMS,
    )(where, mine, arrived)
    return result.reshape(1, C, TILE, W)


def solution(mesh):
    placed = (P("layer", None, "space", None), P("layer", None, None))
    return jax.shard_map(
        on_device,
        mesh=mesh,
        in_specs=placed,
        out_specs=P("layer", None, "space", None),
        check_vma=False,
    )
```

```python
import functools
import jax
import jax.numpy as jnp
from jax import lax
from jax.experimental import pallas as pl
from jax.experimental.pallas import tpu as pltpu
from jax.sharding import PartitionSpec as P

C = 64
W = 128
TILE = 16
GROUP = 8
BAND = 3 * C
RASTER = 128
BF = jnp.bfloat16
F32 = jnp.float32
VM = pl.BlockSpec(memory_space=pltpu.VMEM)
SM = pl.BlockSpec(memory_space=pltpu.SMEM)
PARAMS = pltpu.CompilerParams(vmem_limit_bytes=12 * 1024 * 1024)


def build_band(band, taps):
    for i in range(2):
        band[i * C : (i + 1) * C, i * BAND : (i + 3) * BAND] = taps


def clear_band(band):
    band[...] = jnp.zeros_like(band)


def activate_row(value, acts, q, first_row):
    lane = lax.broadcasted_iota(jnp.int32, (C, W), 1)
    row = first_row + q
    inside = jnp.logical_and(row >= 0, row < RASTER)
    keep = jnp.where(inside, 1.0, 0.0).astype(F32)
    a = (jnp.maximum(value, 0.0) * keep).astype(BF)
    zero = jnp.zeros((), BF)
    base = q * BAND
    acts[base : base + 64, :] = jnp.where(lane == 0, zero, pltpu.roll(a, 1, 1))
    acts[base + 64 : base + 128, :] = a
    acts[base + 128 : base + 192, :] = jnp.where(lane == W - 1, zero, pltpu.roll(a, W - 1, 1))


def activate(state, acts, lo, hi, first_row):
    for q in range(lo, hi):
        activate_row(state[q], acts, q, first_row)


def convolve(band, acts, lo, hi, emit):
    for r in range(lo, hi, 4):
        pair = [q for q in (r, r + 2) if q < hi]
        parts = [acts[(q - 1) * BAND : (q + 3) * BAND, :] for q in pair]
        rhs = parts[0] if len(parts) == 1 else jnp.concatenate(parts, axis=1)
        y = jnp.dot(band[...], rhs, preferred_element_type=F32)
        for n, q in enumerate(pair):
            for i in range(2):
                emit(q + i, y[i * C : (i + 1) * C, n * W : (n + 1) * W])


def prep_kernel(start, tile, top, bot, top4, bot4):
    for h in range(TILE):
        row = start[pl.ds(h, C, stride=TILE), :].astype(BF)
        tile[h] = row
        if h < 8:
            top[h] = row
        else:
            bot[h - 8] = row
        if h < 4:
            top4[h] = row
        if h >= 12:
            bot4[h - 12] = row


def defect_kernel(where, mid, up, down, tile, up4, down4, before, taps, out, state, coarse, acts, acts2, band):
    first_row = where[1] * TILE - 8
    origin = where[0] == 0
    both = (acts, acts2)
    clear_band(band)

    @pl.when(origin)
    def _():
        for h in range(4):
            state[4 + h] = up4[h].astype(F32)
            state[24 + h] = down4[h].astype(F32)
        for h in range(TILE):
            state[8 + h] = tile[h].astype(F32)
        activate(state, acts, 4, 28, first_row)

    @pl.when(jnp.logical_not(origin))
    def _():
        for h in range(8):
            state[h] = up[h].astype(F32)
            state[24 + h] = down[h].astype(F32)
        for h in range(TILE):
            state[8 + h] = mid[h].astype(F32)
        activate(state, acts, 0, 32, first_row)
        for t in range(4):
            build_band(band, before[t])

            def emit(r, y):
                v = state[r] + 0.125 * y
                state[r] = v
                activate_row(v, both[(t + 1) % 2], r, first_row)

            convolve(band, both[t % 2], 1 + t, 31 - t, emit)

    subtract = jnp.where(origin, 0.0, 1.0).astype(F32)
    for t in range(4):
        build_band(band, taps[t])

        def emit(r, y):
            u = state[r]
            v = u + 0.125 * y
            if t == 0 and 8 <= r < 24:
                coarse[r - 8] = (u + 0.5 * y) * subtract
            if t < 3:
                state[r] = v
                activate_row(v, both[(t + 1) % 2], r, first_row)
            else:
                out[r - 8] = (v - coarse[r - 8]).astype(BF)

        convolve(band, both[t % 2], 5 + t, 27 - t, emit)


def slot_of(where, d, swapped):
    x, c = where[2], where[3]
    return 2 * lax.rem(x - d + 4, 4) + (1 - c if swapped else c)


OFFSETS = [0, 7, 13, 18, 22, 25, 27, 28]


def arrange_kernel(where, *refs):
    pieces, ordered, packed = refs[:10], refs[10], refs[11]
    c = where[3]
    places = [(0, 0, 16), (1, 0, 16), (3, 0, 16), (2, 0, 8), (2, 8, 8)]
    for n, (d, begin, count) in enumerate(places):
        for swapped in (0, 1):
            slot = slot_of(where, d, swapped)
            ordered[pl.ds(slot, 1), begin : begin + count] = pieces[2 * n + swapped][...][None]
    for j in range(7):
        count = 7 - j
        begin = jnp.where(c == 0, TILE - count, 0)
        packed[OFFSETS[j] : OFFSETS[j + 1]] = ordered[j, pl.ds(begin, count)]


def coarse_kernel(
    turn, where, ordered, edges, w0, w1, w2, w3, own, other, halo, mine_in, theirs_in,
    sent, mine, theirs, state, acts, acts2, band, past, taps
):
    x, c = where[2], where[3]
    first_row = where[1] * TILE - 8 + 8 * c
    both = (acts, acts2)

    @pl.when(where[4] != turn)
    def _():
        mine[...] = mine_in[...]
        theirs[...] = theirs_in[...]
        sent[...] = jnp.zeros_like(sent)

    @pl.when(where[4] == turn)
    def _():
        clear_band(band)
        def defect_row(j, r):
            if 8 <= r < 16:
                e = ordered[j, r - 8 + 8 * c]
            elif r < 8:
                e = jnp.where(c == 0, edges[OFFSETS[j] + r - 1 - j], ordered[j, r])
            else:
                e = jnp.where(c == 0, ordered[j, r - 8], edges[OFFSETS[j] + r - 16])
            return e.astype(F32)

        if turn == 0:
            for r in range(1, 23):
                v = defect_row(0, r)
                state[r] = v
                activate_row(v, acts2, r, first_row)
                if 8 <= r < 16:
                    past[0, r - 8] = v
        else:
            for h in range(24):
                if h < 8:
                    v = jnp.where(c == 0, halo[h].astype(F32), other[h].astype(F32))
                elif h < 16:
                    v = own[h - 8].astype(F32)
                else:
                    v = jnp.where(c == 0, other[h - 16].astype(F32), halo[h - 16].astype(F32))
                state[h] = v
                activate_row(v, acts, h, first_row)
        for d, pair in enumerate((w0, w1, w2, w3)):
            for swapped in (0, 1):
                taps[slot_of(where, d, swapped)] = pair[swapped]

        for j in range(1 if turn == 0 else 0, GROUP):
            build_band(band, taps[j])

            def emit(r, y):
                v = state[r] + 0.5 * y + defect_row(j, r)
                if j < GROUP - 1:
                    state[r] = v
                    activate_row(v, both[(j + 1) % 2], r, first_row)
                else:
                    sent[r - 8] = v.astype(BF)
                if 8 <= r < 16:
                    past[j, r - 8] = v

            convolve(band, both[j % 2], 1 + j, 23 - j, emit)

        mine[...] = past[2 * x + c]
        theirs[...] = past[2 * x + 1 - c].astype(BF)


def finish_kernel(where, mine, arrived, out):
    c = where[3]

    def put(lo_rows, hi_rows):
        for h in range(8):
            out[pl.ds(h, C, stride=TILE), :] = lo_rows(h)
            out[pl.ds(h + 8, C, stride=TILE), :] = hi_rows(h)

    @pl.when(c == 0)
    def _():
        put(lambda h: mine[h], lambda h: arrived[h].astype(F32))

    @pl.when(c != 0)
    def _():
        put(lambda h: arrived[h].astype(F32), lambda h: mine[h])


def rows_of(n, dtype=BF):
    return jax.ShapeDtypeStruct((n, C, W), dtype)


def on_device(start_values, weights):
    layer = lax.axis_index("layer")
    space = lax.axis_index("space")
    blocks = lax.axis_size("layer")
    tiles = lax.axis_size("space")
    axes = ("layer", "space")
    x = lax.rem(layer, 8) // 2
    c = lax.rem(layer, 2)
    where = jnp.stack([layer, space, x, c, layer // GROUP]).astype(jnp.int32)
    start = start_values.reshape(C * TILE, W)

    def at(l, s):
        return l * tiles + s

    def shifted(piece, dl, ds):
        return lax.ppermute(piece, axes, [(at(l, s), at((l + dl) % blocks, (s + ds) % tiles)) for l, s in everywhere])

    def by_output(taps):
        return taps.reshape(4, 9, C, C).transpose(0, 2, 1, 3).reshape(4, C, 9 * C)

    everywhere = [(l, s) for l in range(blocks) for s in range(tiles)]
    before = shifted(weights, 1, 0)
    tile, top, bot, top4, bot4 = pl.pallas_call(
        prep_kernel,
        out_shape=(rows_of(16), rows_of(8), rows_of(8), rows_of(4), rows_of(4)),
        in_specs=[VM],
        out_specs=(VM,) * 5,
        compiler_params=PARAMS,
    )(start)
    mid = shifted(tile, 1, 0)
    up = shifted(bot, 1, 1)
    down = shifted(top, 1, -1)
    up4 = shifted(bot4, 0, 1)
    down4 = shifted(top4, 0, -1)

    swap = [(l, l ^ 1) for l in range(blocks)]
    before = by_output(before)
    flat = by_output(weights)
    first, mid = lax.optimization_barrier((flat[0], mid))
    pair = jnp.stack([first, lax.ppermute(first, "layer", swap)])

    def around(piece, d, cores=(0, 1)):
        pairs = [(l, l // 8 * 8 + (l % 8 + 2 * d) % 8) for l in range(blocks) if l % 2 in cores]
        return lax.ppermute(piece, "layer", pairs)

    defect = pl.pallas_call(
        defect_kernel,
        out_shape=rows_of(16),
        in_specs=[SM] + [VM] * 8,
        out_specs=VM,
        scratch_shapes=[
            pltpu.VMEM((32, C, W), F32),
            pltpu.VMEM((16, C, W), F32),
            pltpu.VMEM((32 * BAND, W), BF),
            pltpu.VMEM((32 * BAND, W), BF),
            pltpu.VMEM((2 * C, 4 * BAND), BF),
        ],
        cost_estimate=pl.CostEstimate(flops=2_000_000_000, bytes_accessed=4_000_000, transcendentals=0),
        compiler_params=PARAMS,
    )(where, mid, up, down, tile, up4, down4, before, flat)

    ahead = around(defect, 1)
    behind = around(defect, 3)
    across = around(defect[:8], 2)
    across2 = around(behind[8:], 3)
    pieces = []
    for piece in (defect, ahead, behind, across, across2):
        pieces += [piece, lax.ppermute(piece, "layer", swap)]
    ordered, packed = pl.pallas_call(
        arrange_kernel,
        out_shape=(jax.ShapeDtypeStruct((GROUP, TILE, C, W), BF), rows_of(28)),
        in_specs=[SM] + [VM] * 10,
        out_specs=(VM, VM),
        compiler_params=PARAMS,
    )(where, *pieces)
    edge_pairs = [
        (at(l, s), at(l, (s + 1) % tiles if l % 2 == 0 else (s - 1) % tiles)) for l in range(blocks) for s in range(tiles)
    ]
    pair, packed = lax.optimization_barrier((pair, packed))
    edges = lax.ppermute(packed, axes, edge_pairs)
    coarse_taps = [pair, around(pair, 1), around(pair, 2), around(pair, 3)]

    own = other = halo = jnp.zeros((8, C, W), BF)
    mine = jnp.zeros((8, C, W), F32)
    theirs = jnp.zeros((8, C, W), BF)
    turns = blocks // GROUP
    for turn in range(turns):
        sent, mine, theirs = pl.pallas_call(
            functools.partial(coarse_kernel, turn),
            out_shape=(rows_of(8), rows_of(8, F32), rows_of(8)),
            in_specs=[SM] + [VM] * 11,
            out_specs=(VM, VM, VM),
            scratch_shapes=[
                pltpu.VMEM((24, C, W), F32),
                pltpu.VMEM((24 * BAND, W), BF),
                pltpu.VMEM((24 * BAND, W), BF),
                pltpu.VMEM((2 * C, 4 * BAND), BF),
                pltpu.VMEM((GROUP, 8, C, W), F32),
                pltpu.VMEM((GROUP, C, 9 * C), BF),
            ],
            input_output_aliases={10: 1, 11: 2},
            compiler_params=PARAMS,
        )(where, ordered, edges, *coarse_taps, own, other, halo, mine, theirs)
        if turn + 1 < turns:
            own = lax.ppermute(sent, "layer", [(l, (l + 8) % blocks) for l in range(blocks)])
            other = lax.ppermute(own, "layer", swap)
            halo = lax.ppermute(
                sent,
                axes,
                [(at(l, s), at(((l ^ 1) + 8) % blocks, (s + (1 if l % 2 else -1)) % tiles)) for l, s in everywhere],
            )
    arrived = lax.ppermute(theirs, "layer", swap)
    result = pl.pallas_call(
        finish_kernel,
        out_shape=jax.ShapeDtypeStruct((C * TILE, W), F32),
        in_specs=[SM, VM, VM],
        out_specs=VM,
        compiler_params=PARAMS,
    )(where, mine, arrived)
    return result.reshape(1, C, TILE, W)


def solution(mesh):
    placed = (P("layer", None, "space", None), P("layer", None, None))
    return jax.shard_map(
        on_device,
        mesh=mesh,
        in_specs=placed,
        out_specs=P("layer", None, "space", None),
        check_vma=False,
    )
```

```python
import functools
import jax
import jax.numpy as jnp
from jax import lax
from jax.experimental import pallas as pl
from jax.experimental.pallas import tpu as pltpu
from jax.sharding import PartitionSpec as P

C = 64
W = 128
TILE = 16
GROUP = 8
BAND = 3 * C
RASTER = 128
BF = jnp.bfloat16
F32 = jnp.float32
VM = pl.BlockSpec(memory_space=pltpu.VMEM)
SM = pl.BlockSpec(memory_space=pltpu.SMEM)
PARAMS = pltpu.CompilerParams(vmem_limit_bytes=12 * 1024 * 1024)


def build_band(band, taps):
    for i in range(2):
        band[i * C : (i + 1) * C, i * BAND : (i + 3) * BAND] = taps


def clear_band(band):
    band[...] = jnp.zeros_like(band)


def activate_row(value, acts, q, first_row):
    lane = lax.broadcasted_iota(jnp.int32, (C, W), 1)
    row = first_row + q
    inside = jnp.logical_and(row >= 0, row < RASTER)
    keep = jnp.where(inside, 1.0, 0.0).astype(F32)
    a = (jnp.maximum(value, 0.0) * keep).astype(BF)
    zero = jnp.zeros((), BF)
    base = q * BAND
    acts[base : base + 64, :] = jnp.where(lane == 0, zero, pltpu.roll(a, 1, 1))
    acts[base + 64 : base + 128, :] = a
    acts[base + 128 : base + 192, :] = jnp.where(lane == W - 1, zero, pltpu.roll(a, W - 1, 1))


def activate(state, acts, lo, hi, first_row):
    for q in range(lo, hi):
        activate_row(state[q], acts, q, first_row)


def convolve(band, acts, lo, hi, emit):
    for r in range(lo, hi, 4):
        pair = [q for q in (r, r + 2) if q < hi]
        parts = [acts[(q - 1) * BAND : (q + 3) * BAND, :] for q in pair]
        rhs = parts[0] if len(parts) == 1 else jnp.concatenate(parts, axis=1)
        y = jnp.dot(band[...], rhs, preferred_element_type=F32)
        for n, q in enumerate(pair):
            for i in range(2):
                emit(q + i, y[i * C : (i + 1) * C, n * W : (n + 1) * W])


def prep_kernel(start, tile, top, bot, top4, bot4):
    for h in range(TILE):
        row = start[pl.ds(h, C, stride=TILE), :].astype(BF)
        tile[h] = row
        if h < 8:
            top[h] = row
        else:
            bot[h - 8] = row
        if h < 4:
            top4[h] = row
        if h >= 12:
            bot4[h - 12] = row


def defect_kernel(where, mid, up, down, tile, up4, down4, before, taps, out, state, coarse, acts, acts2, band):
    first_row = where[1] * TILE - 8
    origin = where[0] == 0
    both = (acts, acts2)
    clear_band(band)

    @pl.when(origin)
    def _():
        for h in range(4):
            state[4 + h] = up4[h].astype(F32)
            state[24 + h] = down4[h].astype(F32)
        for h in range(TILE):
            state[8 + h] = tile[h].astype(F32)
        activate(state, acts, 4, 28, first_row)

    @pl.when(jnp.logical_not(origin))
    def _():
        for h in range(8):
            state[h] = up[h].astype(F32)
            state[24 + h] = down[h].astype(F32)
        for h in range(TILE):
            state[8 + h] = mid[h].astype(F32)
        activate(state, acts, 0, 32, first_row)
        for t in range(4):
            build_band(band, before[t])

            def emit(r, y):
                v = state[r] + 0.125 * y
                state[r] = v
                activate_row(v, both[(t + 1) % 2], r, first_row)

            convolve(band, both[t % 2], 1 + t, 31 - t, emit)

    subtract = jnp.where(origin, 0.0, 1.0).astype(F32)
    for t in range(4):
        build_band(band, taps[t])

        def emit(r, y):
            u = state[r]
            v = u + 0.125 * y
            if t == 0 and 8 <= r < 24:
                coarse[r - 8] = (u + 0.5 * y) * subtract
            if t < 3:
                state[r] = v
                activate_row(v, both[(t + 1) % 2], r, first_row)
            else:
                out[r - 8] = (v - coarse[r - 8]).astype(BF)

        convolve(band, both[t % 2], 5 + t, 27 - t, emit)


def slot_of(where, d, swapped):
    x, c = where[2], where[3]
    return 2 * lax.rem(x - d + 4, 4) + (1 - c if swapped else c)


OFFSETS = [0, 7, 13, 18, 22, 25, 27, 28]


def arrange_kernel(where, *refs):
    pieces, ordered, packed = refs[:10], refs[10], refs[11]
    c = where[3]
    places = [(0, 0, 16), (1, 0, 16), (3, 0, 16), (2, 0, 8), (2, 8, 8)]
    for n, (d, begin, count) in enumerate(places):
        for swapped in (0, 1):
            slot = slot_of(where, d, swapped)
            ordered[pl.ds(slot, 1), begin : begin + count] = pieces[2 * n + swapped][...][None]
    for j in range(7):
        count = 7 - j
        begin = jnp.where(c == 0, TILE - count, 0)
        packed[OFFSETS[j] : OFFSETS[j + 1]] = ordered[j, pl.ds(begin, count)]


def coarse_kernel(
    turn, where, ordered, edges, w0, w1, w2, w3, own, other, halo, mine_in, theirs_in,
    *refs,
):
    mine, theirs = refs[:2]
    sent = refs[2] if len(refs) == 9 else None
    state, acts, acts2, band, past, taps = refs[-6:]
    x, c = where[2], where[3]
    first_row = where[1] * TILE - 8 + 8 * c
    both = (acts, acts2)

    @pl.when(where[4] != turn)
    def _():
        mine[...] = mine_in[...]
        theirs[...] = theirs_in[...]
        if sent is not None:
            sent[...] = jnp.zeros_like(sent)

    @pl.when(where[4] == turn)
    def _():
        clear_band(band)
        def defect_row(j, r):
            if 8 <= r < 16:
                e = ordered[j, r - 8 + 8 * c]
            elif r < 8:
                e = jnp.where(c == 0, edges[OFFSETS[j] + r - 1 - j], ordered[j, r])
            else:
                e = jnp.where(c == 0, ordered[j, r - 8], edges[OFFSETS[j] + r - 16])
            return e.astype(F32)

        if turn == 0:
            for r in range(1, 23):
                v = defect_row(0, r)
                state[r] = v
                activate_row(v, acts2, r, first_row)
                if 8 <= r < 16:
                    past[0, r - 8] = v
        else:
            for h in range(24):
                if h < 8:
                    v = jnp.where(c == 0, halo[h].astype(F32), other[h].astype(F32))
                elif h < 16:
                    v = own[h - 8].astype(F32)
                else:
                    v = jnp.where(c == 0, other[h - 16].astype(F32), halo[h - 16].astype(F32))
                state[h] = v
                activate_row(v, acts, h, first_row)
        for d, pair in enumerate((w0, w1, w2, w3)):
            for swapped in (0, 1):
                taps[slot_of(where, d, swapped)] = pair[swapped]

        for j in range(1 if turn == 0 else 0, GROUP):
            build_band(band, taps[j])

            def emit(r, y):
                v = state[r] + 0.5 * y + defect_row(j, r)
                if j < GROUP - 1:
                    state[r] = v
                    activate_row(v, both[(j + 1) % 2], r, first_row)
                elif sent is not None:
                    sent[r - 8] = v.astype(BF)
                if 8 <= r < 16:
                    past[j, r - 8] = v

            convolve(band, both[j % 2], 1 + j, 23 - j, emit)

        mine[...] = past[2 * x + c]
        theirs[...] = past[2 * x + 1 - c].astype(BF)


def finish_kernel(where, mine, arrived, out):
    c = where[3]

    def put(lo_rows, hi_rows):
        for h in range(8):
            out[pl.ds(h, C, stride=TILE), :] = lo_rows(h)
            out[pl.ds(h + 8, C, stride=TILE), :] = hi_rows(h)

    @pl.when(c == 0)
    def _():
        put(lambda h: mine[h], lambda h: arrived[h].astype(F32))

    @pl.when(c != 0)
    def _():
        put(lambda h: arrived[h].astype(F32), lambda h: mine[h])


def rows_of(n, dtype=BF):
    return jax.ShapeDtypeStruct((n, C, W), dtype)


def on_device(start_values, weights):
    layer = lax.axis_index("layer")
    space = lax.axis_index("space")
    blocks = lax.axis_size("layer")
    tiles = lax.axis_size("space")
    axes = ("layer", "space")
    x = lax.rem(layer, 8) // 2
    c = lax.rem(layer, 2)
    where = jnp.stack([layer, space, x, c, layer // GROUP]).astype(jnp.int32)
    start = start_values.reshape(C * TILE, W)

    def at(l, s):
        return l * tiles + s

    def shifted(piece, dl, ds):
        return lax.ppermute(piece, axes, [(at(l, s), at((l + dl) % blocks, (s + ds) % tiles)) for l, s in everywhere])

    def by_output(taps):
        return taps.reshape(4, 9, C, C).transpose(0, 2, 1, 3).reshape(4, C, 9 * C)

    everywhere = [(l, s) for l in range(blocks) for s in range(tiles)]
    before = shifted(weights, 1, 0)
    tile, top, bot, top4, bot4 = pl.pallas_call(
        prep_kernel,
        out_shape=(rows_of(16), rows_of(8), rows_of(8), rows_of(4), rows_of(4)),
        in_specs=[VM],
        out_specs=(VM,) * 5,
        compiler_params=PARAMS,
    )(start)
    mid = shifted(tile, 1, 0)
    up = shifted(bot, 1, 1)
    down = shifted(top, 1, -1)
    up4 = shifted(bot4, 0, 1)
    down4 = shifted(top4, 0, -1)

    swap = [(l, l ^ 1) for l in range(blocks)]
    before = by_output(before)
    flat = by_output(weights)
    first, mid = lax.optimization_barrier((flat[0], mid))
    pair = jnp.stack([first, lax.ppermute(first, "layer", swap)])

    def around(piece, d, cores=(0, 1)):
        pairs = [(l, l // 8 * 8 + (l % 8 + 2 * d) % 8) for l in range(blocks) if l % 2 in cores]
        return lax.ppermute(piece, "layer", pairs)

    defect = pl.pallas_call(
        defect_kernel,
        out_shape=rows_of(16),
        in_specs=[SM] + [VM] * 8,
        out_specs=VM,
        scratch_shapes=[
            pltpu.VMEM((32, C, W), F32),
            pltpu.VMEM((16, C, W), F32),
            pltpu.VMEM((32 * BAND, W), BF),
            pltpu.VMEM((32 * BAND, W), BF),
            pltpu.VMEM((2 * C, 4 * BAND), BF),
        ],
        cost_estimate=pl.CostEstimate(flops=2_000_000_000, bytes_accessed=4_000_000, transcendentals=0),
        compiler_params=PARAMS,
    )(where, mid, up, down, tile, up4, down4, before, flat)

    ahead = around(defect, 1)
    behind = around(defect, 3)
    across = around(defect[:8], 2)
    across2 = around(behind[8:], 3)
    pieces = []
    for piece in (defect, ahead, behind, across, across2):
        pieces += [piece, lax.ppermute(piece, "layer", swap)]
    ordered, packed = pl.pallas_call(
        arrange_kernel,
        out_shape=(jax.ShapeDtypeStruct((GROUP, TILE, C, W), BF), rows_of(28)),
        in_specs=[SM] + [VM] * 10,
        out_specs=(VM, VM),
        compiler_params=PARAMS,
    )(where, *pieces)
    edge_pairs = [
        (at(l, s), at(l, (s + 1) % tiles if l % 2 == 0 else (s - 1) % tiles)) for l in range(blocks) for s in range(tiles)
    ]
    pair, packed = lax.optimization_barrier((pair, packed))
    edges = lax.ppermute(packed, axes, edge_pairs)
    coarse_taps = [pair, around(pair, 1), around(pair, 2), around(pair, 3)]

    own = other = halo = jnp.zeros((8, C, W), BF)
    mine = jnp.zeros((8, C, W), F32)
    theirs = jnp.zeros((8, C, W), BF)
    turns = blocks // GROUP
    for turn in range(turns):
        last = turn + 1 == turns
        mine, theirs, *sent = pl.pallas_call(
            functools.partial(coarse_kernel, turn),
            out_shape=(rows_of(8, F32), rows_of(8)) + (() if last else (rows_of(8),)),
            in_specs=[SM] + [VM] * 11,
            out_specs=(VM,) * (2 if last else 3),
            scratch_shapes=[
                pltpu.VMEM((24, C, W), F32),
                pltpu.VMEM((24 * BAND, W), BF),
                pltpu.VMEM((24 * BAND, W), BF),
                pltpu.VMEM((2 * C, 4 * BAND), BF),
                pltpu.VMEM((GROUP, 8, C, W), F32),
                pltpu.VMEM((GROUP, C, 9 * C), BF),
            ],
            input_output_aliases={10: 0, 11: 1},
            compiler_params=PARAMS,
        )(where, ordered, edges, *coarse_taps, own, other, halo, mine, theirs)
        if not last:
            sent = sent[0]
            own = lax.ppermute(sent, "layer", [(l, (l + 8) % blocks) for l in range(blocks)])
            other = lax.ppermute(own, "layer", swap)
            halo = lax.ppermute(
                sent,
                axes,
                [(at(l, s), at(((l ^ 1) + 8) % blocks, (s + (1 if l % 2 else -1)) % tiles)) for l, s in everywhere],
            )
    arrived = lax.ppermute(theirs, "layer", swap)
    result = pl.pallas_call(
        finish_kernel,
        out_shape=jax.ShapeDtypeStruct((C * TILE, W), F32),
        in_specs=[SM, VM, VM],
        out_specs=VM,
        compiler_params=PARAMS,
    )(where, mine, arrived)
    return result.reshape(1, C, TILE, W)


def solution(mesh):
    placed = (P("layer", None, "space", None), P("layer", None, None))
    return jax.shard_map(
        on_device,
        mesh=mesh,
        in_specs=placed,
        out_specs=P("layer", None, "space", None),
        check_vma=False,
    )
```

```python
import functools
import jax
import jax.numpy as jnp
from jax import lax
from jax.experimental import pallas as pl
from jax.experimental.pallas import tpu as pltpu
from jax.sharding import PartitionSpec as P

C = 64
W = 128
TILE = 16
GROUP = 8
BAND = 3 * C
RASTER = 128
BF = jnp.bfloat16
F32 = jnp.float32
VM = pl.BlockSpec(memory_space=pltpu.VMEM)
PARAMS = pltpu.CompilerParams(vmem_limit_bytes=12 * 1024 * 1024)


def build_band(band, taps):
    for i in range(2):
        band[i * C : (i + 1) * C, i * BAND : (i + 3) * BAND] = taps


def clear_band(band):
    band[...] = jnp.zeros_like(band)


def activate_row(value, acts, q, first_row):
    lane = lax.broadcasted_iota(jnp.int32, (C, W), 1)
    row = first_row + q
    inside = jnp.logical_and(row >= 0, row < RASTER)
    keep = jnp.where(inside, 1.0, 0.0).astype(F32)
    a = (jnp.maximum(value, 0.0) * keep).astype(BF)
    zero = jnp.zeros((), BF)
    base = q * BAND
    acts[base : base + 64, :] = jnp.where(lane == 0, zero, pltpu.roll(a, 1, 1))
    acts[base + 64 : base + 128, :] = a
    acts[base + 128 : base + 192, :] = jnp.where(lane == W - 1, zero, pltpu.roll(a, W - 1, 1))


def activate(state, acts, lo, hi, first_row):
    for q in range(lo, hi):
        activate_row(state[q], acts, q, first_row)


def convolve(band, acts, lo, hi, emit):
    for r in range(lo, hi, 4):
        pair = [q for q in (r, r + 2) if q < hi]
        parts = [acts[(q - 1) * BAND : (q + 3) * BAND, :] for q in pair]
        rhs = parts[0] if len(parts) == 1 else jnp.concatenate(parts, axis=1)
        y = jnp.dot(band[...], rhs, preferred_element_type=F32)
        for n, q in enumerate(pair):
            for i in range(2):
                emit(q + i, y[i * C : (i + 1) * C, n * W : (n + 1) * W])


def prep_kernel(start, tile, top, bot, top4, bot4):
    for h in range(TILE):
        row = start[pl.ds(h, C, stride=TILE), :].astype(BF)
        tile[h] = row
        if h < 8:
            top[h] = row
        else:
            bot[h - 8] = row
        if h < 4:
            top4[h] = row
        if h >= 12:
            bot4[h - 12] = row


def defect_kernel(mid, up, down, tile, up4, down4, before, taps, out, state, coarse, acts, acts2, band):
    where = position()
    first_row = where[1] * TILE - 8
    origin = where[0] == 0
    both = (acts, acts2)
    clear_band(band)

    @pl.when(origin)
    def _():
        for h in range(4):
            state[4 + h] = up4[h].astype(F32)
            state[24 + h] = down4[h].astype(F32)
        for h in range(TILE):
            state[8 + h] = tile[h].astype(F32)
        activate(state, acts, 4, 28, first_row)

    @pl.when(jnp.logical_not(origin))
    def _():
        for h in range(8):
            state[h] = up[h].astype(F32)
            state[24 + h] = down[h].astype(F32)
        for h in range(TILE):
            state[8 + h] = mid[h].astype(F32)
        activate(state, acts, 0, 32, first_row)
        for t in range(4):
            build_band(band, before[t])

            def emit(r, y):
                v = state[r] + 0.125 * y
                state[r] = v
                activate_row(v, both[(t + 1) % 2], r, first_row)

            convolve(band, both[t % 2], 1 + t, 31 - t, emit)

    subtract = jnp.where(origin, 0.0, 1.0).astype(F32)
    for t in range(4):
        build_band(band, taps[t])

        def emit(r, y):
            u = state[r]
            v = u + 0.125 * y
            if t == 0 and 8 <= r < 24:
                coarse[r - 8] = (u + 0.5 * y) * subtract
            if t < 3:
                state[r] = v
                activate_row(v, both[(t + 1) % 2], r, first_row)
            else:
                out[r - 8] = (v - coarse[r - 8]).astype(BF)

        convolve(band, both[t % 2], 5 + t, 27 - t, emit)


def position():
    layer, space = lax.axis_index("layer"), lax.axis_index("space")
    return layer, space, lax.rem(layer, GROUP) // 2, lax.rem(layer, 2), layer // GROUP


def slot_of(where, d, swapped):
    x, c = where[2], where[3]
    return 2 * lax.rem(x - d + 4, 4) + (1 - c if swapped else c)


OFFSETS = [0, 7, 13, 18, 22, 25, 27, 28]


def arrange_kernel(*refs):
    where = position()
    pieces, ordered, packed = refs[:10], refs[10], refs[11]
    c = where[3]
    places = [(0, 0, 16), (1, 0, 16), (3, 0, 16), (2, 0, 8), (2, 8, 8)]
    for n, (d, begin, count) in enumerate(places):
        for swapped in (0, 1):
            slot = slot_of(where, d, swapped)
            ordered[pl.ds(slot, 1), begin : begin + count] = pieces[2 * n + swapped][...][None]
    for j in range(7):
        count = 7 - j
        begin = jnp.where(c == 0, TILE - count, 0)
        packed[OFFSETS[j] : OFFSETS[j + 1]] = ordered[j, pl.ds(begin, count)]


def coarse_kernel(
    turn, ordered, edges, w0, w1, w2, w3, own, other, halo, mine_in, theirs_in,
    *refs,
):
    where = position()
    mine, theirs = refs[:2]
    sent = refs[2] if len(refs) == 9 else None
    state, acts, acts2, band, past, taps = refs[-6:]
    x, c = where[2], where[3]
    first_row = where[1] * TILE - 8 + 8 * c
    both = (acts, acts2)

    @pl.when(where[4] != turn)
    def _():
        mine[...] = mine_in[...]
        theirs[...] = theirs_in[...]
        if sent is not None:
            sent[...] = jnp.zeros_like(sent)

    @pl.when(where[4] == turn)
    def _():
        clear_band(band)
        def defect_row(j, r):
            if 8 <= r < 16:
                e = ordered[j, r - 8 + 8 * c]
            elif r < 8:
                e = jnp.where(c == 0, edges[OFFSETS[j] + r - 1 - j], ordered[j, r])
            else:
                e = jnp.where(c == 0, ordered[j, r - 8], edges[OFFSETS[j] + r - 16])
            return e.astype(F32)

        if turn == 0:
            for r in range(1, 23):
                v = defect_row(0, r)
                state[r] = v
                activate_row(v, acts2, r, first_row)
                if 8 <= r < 16:
                    past[0, r - 8] = v
        else:
            for h in range(24):
                if h < 8:
                    v = jnp.where(c == 0, halo[h].astype(F32), other[h].astype(F32))
                elif h < 16:
                    v = own[h - 8].astype(F32)
                else:
                    v = jnp.where(c == 0, other[h - 16].astype(F32), halo[h - 16].astype(F32))
                state[h] = v
                activate_row(v, acts, h, first_row)
        for d, pair in enumerate((w0, w1, w2, w3)):
            for swapped in (0, 1):
                taps[slot_of(where, d, swapped)] = pair[swapped]

        for j in range(1 if turn == 0 else 0, GROUP):
            build_band(band, taps[j])

            def emit(r, y):
                v = state[r] + 0.5 * y + defect_row(j, r)
                if j < GROUP - 1:
                    state[r] = v
                    activate_row(v, both[(j + 1) % 2], r, first_row)
                elif sent is not None:
                    sent[r - 8] = v.astype(BF)
                if 8 <= r < 16:
                    past[j, r - 8] = v

            convolve(band, both[j % 2], 1 + j, 23 - j, emit)

        mine[...] = past[2 * x + c]
        theirs[...] = past[2 * x + 1 - c].astype(BF)


def finish_kernel(mine, arrived, out):
    where = position()
    c = where[3]

    def put(lo_rows, hi_rows):
        for h in range(8):
            out[pl.ds(h, C, stride=TILE), :] = lo_rows(h)
            out[pl.ds(h + 8, C, stride=TILE), :] = hi_rows(h)

    @pl.when(c == 0)
    def _():
        put(lambda h: mine[h], lambda h: arrived[h].astype(F32))

    @pl.when(c != 0)
    def _():
        put(lambda h: arrived[h].astype(F32), lambda h: mine[h])


def rows_of(n, dtype=BF):
    return jax.ShapeDtypeStruct((n, C, W), dtype)


def on_device(start_values, weights):
    blocks = lax.axis_size("layer")
    tiles = lax.axis_size("space")
    axes = ("layer", "space")
    start = start_values.reshape(C * TILE, W)

    def at(l, s):
        return l * tiles + s

    def shifted(piece, dl, ds):
        return lax.ppermute(piece, axes, [(at(l, s), at((l + dl) % blocks, (s + ds) % tiles)) for l, s in everywhere])

    def by_output(taps):
        return taps.reshape(4, 9, C, C).transpose(0, 2, 1, 3).reshape(4, C, 9 * C)

    everywhere = [(l, s) for l in range(blocks) for s in range(tiles)]
    before = shifted(weights, 1, 0)
    tile, top, bot, top4, bot4 = pl.pallas_call(
        prep_kernel,
        out_shape=(rows_of(16), rows_of(8), rows_of(8), rows_of(4), rows_of(4)),
        in_specs=[VM],
        out_specs=(VM,) * 5,
        compiler_params=PARAMS,
    )(start)
    mid = shifted(tile, 1, 0)
    up = shifted(bot, 1, 1)
    down = shifted(top, 1, -1)
    up4 = shifted(bot4, 0, 1)
    down4 = shifted(top4, 0, -1)

    swap = [(l, l ^ 1) for l in range(blocks)]
    before = by_output(before)
    flat = by_output(weights)
    first, mid = lax.optimization_barrier((flat[0], mid))
    pair = jnp.stack([first, lax.ppermute(first, "layer", swap)])

    def around(piece, d, cores=(0, 1)):
        pairs = [(l, l // 8 * 8 + (l % 8 + 2 * d) % 8) for l in range(blocks) if l % 2 in cores]
        return lax.ppermute(piece, "layer", pairs)

    defect = pl.pallas_call(
        defect_kernel,
        out_shape=rows_of(16),
        in_specs=[VM] * 8,
        out_specs=VM,
        scratch_shapes=[
            pltpu.VMEM((32, C, W), F32),
            pltpu.VMEM((16, C, W), F32),
            pltpu.VMEM((32 * BAND, W), BF),
            pltpu.VMEM((32 * BAND, W), BF),
            pltpu.VMEM((2 * C, 4 * BAND), BF),
        ],
        cost_estimate=pl.CostEstimate(flops=2_000_000_000, bytes_accessed=4_000_000, transcendentals=0),
        compiler_params=PARAMS,
    )(mid, up, down, tile, up4, down4, before, flat)

    ahead = around(defect, 1)
    behind = around(defect, 3)
    across = around(defect[:8], 2)
    across2 = around(behind[8:], 3)
    pieces = []
    for piece in (defect, ahead, behind, across, across2):
        pieces += [piece, lax.ppermute(piece, "layer", swap)]
    ordered, packed = pl.pallas_call(
        arrange_kernel,
        out_shape=(jax.ShapeDtypeStruct((GROUP, TILE, C, W), BF), rows_of(28)),
        in_specs=[VM] * 10,
        out_specs=(VM, VM),
        compiler_params=PARAMS,
    )(*pieces)
    edge_pairs = [
        (at(l, s), at(l, (s + 1) % tiles if l % 2 == 0 else (s - 1) % tiles)) for l in range(blocks) for s in range(tiles)
    ]
    pair, packed = lax.optimization_barrier((pair, packed))
    edges = lax.ppermute(packed, axes, edge_pairs)
    coarse_taps = [pair, around(pair, 1), around(pair, 2), around(pair, 3)]

    own = other = halo = jnp.zeros((8, C, W), BF)
    mine = jnp.zeros((8, C, W), F32)
    theirs = jnp.zeros((8, C, W), BF)
    turns = blocks // GROUP
    for turn in range(turns):
        last = turn + 1 == turns
        mine, theirs, *sent = pl.pallas_call(
            functools.partial(coarse_kernel, turn),
            out_shape=(rows_of(8, F32), rows_of(8)) + (() if last else (rows_of(8),)),
            in_specs=[VM] * 11,
            out_specs=(VM,) * (2 if last else 3),
            scratch_shapes=[
                pltpu.VMEM((24, C, W), F32),
                pltpu.VMEM((24 * BAND, W), BF),
                pltpu.VMEM((24 * BAND, W), BF),
                pltpu.VMEM((2 * C, 4 * BAND), BF),
                pltpu.VMEM((GROUP, 8, C, W), F32),
                pltpu.VMEM((GROUP, C, 9 * C), BF),
            ],
            input_output_aliases={9: 0, 10: 1},
            compiler_params=PARAMS,
        )(ordered, edges, *coarse_taps, own, other, halo, mine, theirs)
        if not last:
            sent = sent[0]
            own = lax.ppermute(sent, "layer", [(l, (l + 8) % blocks) for l in range(blocks)])
            other = lax.ppermute(own, "layer", swap)
            halo = lax.ppermute(
                sent,
                axes,
                [(at(l, s), at(((l ^ 1) + 8) % blocks, (s + (1 if l % 2 else -1)) % tiles)) for l, s in everywhere],
            )
    arrived = lax.ppermute(theirs, "layer", swap)
    result = pl.pallas_call(
        finish_kernel,
        out_shape=jax.ShapeDtypeStruct((C * TILE, W), F32),
        in_specs=[VM, VM],
        out_specs=VM,
        compiler_params=PARAMS,
    )(mine, arrived)
    return result.reshape(1, C, TILE, W)


def solution(mesh):
    placed = (P("layer", None, "space", None), P("layer", None, None))
    return jax.shard_map(
        on_device,
        mesh=mesh,
        in_specs=placed,
        out_specs=P("layer", None, "space", None),
        check_vma=False,
    )
```

```python
import functools
import jax
import jax.numpy as jnp
from jax import lax
from jax.experimental import pallas as pl
from jax.experimental.pallas import tpu as pltpu
from jax.sharding import PartitionSpec as P

C = 64
W = 128
TILE = 16
GROUP = 8
BAND = 3 * C
RASTER = 128
BF = jnp.bfloat16
F32 = jnp.float32
VM = pl.BlockSpec(memory_space=pltpu.VMEM)
PARAMS = pltpu.CompilerParams(vmem_limit_bytes=12 * 1024 * 1024)


def build_band(band, taps):
    for i in range(2):
        band[i * C : (i + 1) * C, i * BAND : (i + 3) * BAND] = taps


def clear_band(band):
    band[...] = jnp.zeros_like(band)


def activate_row(value, acts, q, first_row):
    lane = lax.broadcasted_iota(jnp.int32, (C, W), 1)
    row = first_row + q
    inside = jnp.logical_and(row >= 0, row < RASTER)
    keep = jnp.where(inside, 1.0, 0.0).astype(F32)
    a = (jnp.maximum(value, 0.0) * keep).astype(BF)
    zero = jnp.zeros((), BF)
    base = q * BAND
    acts[base : base + 64, :] = jnp.where(lane == 0, zero, pltpu.roll(a, 1, 1))
    acts[base + 64 : base + 128, :] = a
    acts[base + 128 : base + 192, :] = jnp.where(lane == W - 1, zero, pltpu.roll(a, W - 1, 1))


def activate(state, acts, lo, hi, first_row):
    for q in range(lo, hi):
        activate_row(state[q], acts, q, first_row)


def convolve(band, acts, lo, hi, emit):
    for r in range(lo, hi, 4):
        pair = [q for q in (r, r + 2) if q < hi]
        parts = [acts[(q - 1) * BAND : (q + 3) * BAND, :] for q in pair]
        rhs = parts[0] if len(parts) == 1 else jnp.concatenate(parts, axis=1)
        y = jnp.dot(band[...], rhs, preferred_element_type=F32)
        for n, q in enumerate(pair):
            for i in range(2):
                emit(q + i, y[i * C : (i + 1) * C, n * W : (n + 1) * W])


def prep_kernel(source, tile, top, bot, top4, bot4, start, sems):
    parts = [pl.ds(n * 256, 256) for n in range(4)]
    copies = [pltpu.make_async_copy(source.at[p], start.at[p], sems.at[n]) for n, p in enumerate(parts)]
    for copy in copies:
        copy.start()
    for copy in copies:
        copy.wait()
    for h in range(TILE):
        row = start[pl.ds(h, C, stride=TILE), :].astype(BF)
        tile[h] = row
        if h < 8:
            top[h] = row
        else:
            bot[h - 8] = row
        if h < 4:
            top4[h] = row
        if h >= 12:
            bot4[h - 12] = row


def defect_kernel(mid, up, down, tile, up4, down4, before, taps, out, state, coarse, acts, acts2, band):
    where = position()
    first_row = where[1] * TILE - 8
    origin = where[0] == 0
    both = (acts, acts2)
    clear_band(band)

    @pl.when(origin)
    def _():
        for h in range(4):
            state[4 + h] = up4[h].astype(F32)
            state[24 + h] = down4[h].astype(F32)
        for h in range(TILE):
            state[8 + h] = tile[h].astype(F32)
        activate(state, acts, 4, 28, first_row)

    @pl.when(jnp.logical_not(origin))
    def _():
        for h in range(8):
            state[h] = up[h].astype(F32)
            state[24 + h] = down[h].astype(F32)
        for h in range(TILE):
            state[8 + h] = mid[h].astype(F32)
        activate(state, acts, 0, 32, first_row)
        for t in range(4):
            build_band(band, before[t])

            def emit(r, y):
                v = state[r] + 0.125 * y
                state[r] = v
                activate_row(v, both[(t + 1) % 2], r, first_row)

            convolve(band, both[t % 2], 1 + t, 31 - t, emit)

    subtract = jnp.where(origin, 0.0, 1.0).astype(F32)
    for t in range(4):
        build_band(band, taps[t])

        def emit(r, y):
            u = state[r]
            v = u + 0.125 * y
            if t == 0 and 8 <= r < 24:
                coarse[r - 8] = (u + 0.5 * y) * subtract
            if t < 3:
                state[r] = v
                activate_row(v, both[(t + 1) % 2], r, first_row)
            else:
                out[r - 8] = (v - coarse[r - 8]).astype(BF)

        convolve(band, both[t % 2], 5 + t, 27 - t, emit)


def position():
    layer, space = lax.axis_index("layer"), lax.axis_index("space")
    return layer, space, lax.rem(layer, GROUP) // 2, lax.rem(layer, 2), layer // GROUP


def slot_of(where, d, swapped):
    x, c = where[2], where[3]
    return 2 * lax.rem(x - d + 4, 4) + (1 - c if swapped else c)


OFFSETS = [0, 7, 13, 18, 22, 25, 27, 28]


def arrange_kernel(*refs):
    where = position()
    pieces, ordered, packed = refs[:10], refs[10], refs[11]
    c = where[3]
    places = [(0, 0, 16), (1, 0, 16), (3, 0, 16), (2, 0, 8), (2, 8, 8)]
    for n, (d, begin, count) in enumerate(places):
        for swapped in (0, 1):
            slot = slot_of(where, d, swapped)
            ordered[pl.ds(slot, 1), begin : begin + count] = pieces[2 * n + swapped][...][None]
    for j in range(7):
        count = 7 - j
        begin = jnp.where(c == 0, TILE - count, 0)
        packed[OFFSETS[j] : OFFSETS[j + 1]] = ordered[j, pl.ds(begin, count)]


def coarse_kernel(
    turn, ordered, edges, w0, w1, w2, w3, own, other, halo, mine_in, theirs_in,
    *refs,
):
    where = position()
    mine, theirs = refs[:2]
    sent = refs[2] if len(refs) == 9 else None
    state, acts, acts2, band, past, taps = refs[-6:]
    x, c = where[2], where[3]
    first_row = where[1] * TILE - 8 + 8 * c
    both = (acts, acts2)

    @pl.when(where[4] != turn)
    def _():
        mine[...] = mine_in[...]
        theirs[...] = theirs_in[...]
        if sent is not None:
            sent[...] = jnp.zeros_like(sent)

    @pl.when(where[4] == turn)
    def _():
        clear_band(band)
        def defect_row(j, r):
            if 8 <= r < 16:
                e = ordered[j, r - 8 + 8 * c]
            elif r < 8:
                e = jnp.where(c == 0, edges[OFFSETS[j] + r - 1 - j], ordered[j, r])
            else:
                e = jnp.where(c == 0, ordered[j, r - 8], edges[OFFSETS[j] + r - 16])
            return e.astype(F32)

        if turn == 0:
            for r in range(1, 23):
                v = defect_row(0, r)
                state[r] = v
                activate_row(v, acts2, r, first_row)
                if 8 <= r < 16:
                    past[0, r - 8] = v
        else:
            for h in range(24):
                if h < 8:
                    v = jnp.where(c == 0, halo[h].astype(F32), other[h].astype(F32))
                elif h < 16:
                    v = own[h - 8].astype(F32)
                else:
                    v = jnp.where(c == 0, other[h - 16].astype(F32), halo[h - 16].astype(F32))
                state[h] = v
                activate_row(v, acts, h, first_row)
        for d, pair in enumerate((w0, w1, w2, w3)):
            for swapped in (0, 1):
                taps[slot_of(where, d, swapped)] = pair[swapped]

        for j in range(1 if turn == 0 else 0, GROUP):
            build_band(band, taps[j])

            def emit(r, y):
                v = state[r] + 0.5 * y + defect_row(j, r)
                if j < GROUP - 1:
                    state[r] = v
                    activate_row(v, both[(j + 1) % 2], r, first_row)
                elif sent is not None:
                    sent[r - 8] = v.astype(BF)
                if 8 <= r < 16:
                    past[j, r - 8] = v

            convolve(band, both[j % 2], 1 + j, 23 - j, emit)

        mine[...] = past[2 * x + c]
        theirs[...] = past[2 * x + 1 - c].astype(BF)


def finish_kernel(mine, arrived, out):
    where = position()
    c = where[3]

    def put(lo_rows, hi_rows):
        for h in range(8):
            out[pl.ds(h, C, stride=TILE), :] = lo_rows(h)
            out[pl.ds(h + 8, C, stride=TILE), :] = hi_rows(h)

    @pl.when(c == 0)
    def _():
        put(lambda h: mine[h], lambda h: arrived[h].astype(F32))

    @pl.when(c != 0)
    def _():
        put(lambda h: arrived[h].astype(F32), lambda h: mine[h])


def rows_of(n, dtype=BF):
    return jax.ShapeDtypeStruct((n, C, W), dtype)


def on_device(start_values, weights):
    blocks = lax.axis_size("layer")
    tiles = lax.axis_size("space")
    axes = ("layer", "space")
    start = start_values.reshape(C * TILE, W)

    def at(l, s):
        return l * tiles + s

    def shifted(piece, dl, ds):
        return lax.ppermute(piece, axes, [(at(l, s), at((l + dl) % blocks, (s + ds) % tiles)) for l, s in everywhere])

    def by_output(taps):
        return taps.reshape(4, 9, C, C).transpose(0, 2, 1, 3).reshape(4, C, 9 * C)

    everywhere = [(l, s) for l in range(blocks) for s in range(tiles)]
    before = shifted(weights, 1, 0)
    tile, top, bot, top4, bot4 = pl.pallas_call(
        prep_kernel,
        out_shape=(rows_of(16), rows_of(8), rows_of(8), rows_of(4), rows_of(4)),
        in_specs=[pl.BlockSpec(memory_space=pl.ANY)],
        out_specs=(VM,) * 5,
        scratch_shapes=[pltpu.VMEM((C * TILE, W), F32), pltpu.SemaphoreType.DMA((4,))],
        compiler_params=PARAMS,
    )(start)
    mid = shifted(tile, 1, 0)
    up = shifted(bot, 1, 1)
    down = shifted(top, 1, -1)
    up4 = shifted(bot4, 0, 1)
    down4 = shifted(top4, 0, -1)

    swap = [(l, l ^ 1) for l in range(blocks)]
    before = by_output(before)
    flat = by_output(weights)
    first, mid = lax.optimization_barrier((flat[0], mid))
    pair = jnp.stack([first, lax.ppermute(first, "layer", swap)])

    def around(piece, d, cores=(0, 1)):
        pairs = [(l, l // 8 * 8 + (l % 8 + 2 * d) % 8) for l in range(blocks) if l % 2 in cores]
        return lax.ppermute(piece, "layer", pairs)

    defect = pl.pallas_call(
        defect_kernel,
        out_shape=rows_of(16),
        in_specs=[VM] * 8,
        out_specs=VM,
        scratch_shapes=[
            pltpu.VMEM((32, C, W), F32),
            pltpu.VMEM((16, C, W), F32),
            pltpu.VMEM((32 * BAND, W), BF),
            pltpu.VMEM((32 * BAND, W), BF),
            pltpu.VMEM((2 * C, 4 * BAND), BF),
        ],
        cost_estimate=pl.CostEstimate(flops=2_000_000_000, bytes_accessed=4_000_000, transcendentals=0),
        compiler_params=PARAMS,
    )(mid, up, down, tile, up4, down4, before, flat)

    ahead = around(defect, 1)
    behind = around(defect, 3)
    across = around(defect[:8], 2)
    across2 = around(behind[8:], 3)
    pieces = []
    for piece in (defect, ahead, behind, across, across2):
        pieces += [piece, lax.ppermute(piece, "layer", swap)]
    ordered, packed = pl.pallas_call(
        arrange_kernel,
        out_shape=(jax.ShapeDtypeStruct((GROUP, TILE, C, W), BF), rows_of(28)),
        in_specs=[VM] * 10,
        out_specs=(VM, VM),
        compiler_params=PARAMS,
    )(*pieces)
    edge_pairs = [
        (at(l, s), at(l, (s + 1) % tiles if l % 2 == 0 else (s - 1) % tiles)) for l in range(blocks) for s in range(tiles)
    ]
    pair, packed = lax.optimization_barrier((pair, packed))
    edges = lax.ppermute(packed, axes, edge_pairs)
    coarse_taps = [pair, around(pair, 1), around(pair, 2), around(pair, 3)]

    own = other = halo = jnp.zeros((8, C, W), BF)
    mine = jnp.zeros((8, C, W), F32)
    theirs = jnp.zeros((8, C, W), BF)
    turns = blocks // GROUP
    for turn in range(turns):
        last = turn + 1 == turns
        mine, theirs, *sent = pl.pallas_call(
            functools.partial(coarse_kernel, turn),
            out_shape=(rows_of(8, F32), rows_of(8)) + (() if last else (rows_of(8),)),
            in_specs=[VM] * 11,
            out_specs=(VM,) * (2 if last else 3),
            scratch_shapes=[
                pltpu.VMEM((24, C, W), F32),
                pltpu.VMEM((24 * BAND, W), BF),
                pltpu.VMEM((24 * BAND, W), BF),
                pltpu.VMEM((2 * C, 4 * BAND), BF),
                pltpu.VMEM((GROUP, 8, C, W), F32),
                pltpu.VMEM((GROUP, C, 9 * C), BF),
            ],
            input_output_aliases={9: 0, 10: 1},
            compiler_params=PARAMS,
        )(ordered, edges, *coarse_taps, own, other, halo, mine, theirs)
        if not last:
            sent = sent[0]
            own = lax.ppermute(sent, "layer", [(l, (l + 8) % blocks) for l in range(blocks)])
            other = lax.ppermute(own, "layer", swap)
            halo = lax.ppermute(
                sent,
                axes,
                [(at(l, s), at(((l ^ 1) + 8) % blocks, (s + (1 if l % 2 else -1)) % tiles)) for l, s in everywhere],
            )
    arrived = lax.ppermute(theirs, "layer", swap)
    result = pl.pallas_call(
        finish_kernel,
        out_shape=jax.ShapeDtypeStruct((C * TILE, W), F32),
        in_specs=[VM, VM],
        out_specs=VM,
        compiler_params=PARAMS,
    )(mine, arrived)
    return result.reshape(1, C, TILE, W)


def solution(mesh):
    placed = (P("layer", None, "space", None), P("layer", None, None))
    return jax.shard_map(
        on_device,
        mesh=mesh,
        in_specs=placed,
        out_specs=P("layer", None, "space", None),
        check_vma=False,
    )
```
